512 devices in a mesh: leaf: 64 (over x, z), front: 8 (over y, core).
Axes of the slice: x: 4, y: 4, z: 16, core: 2. Of those that a mesh axis runs over, the one named last changes fastest.
Arguments:
- added_rows: int32 [30, 8, 1], replicated, may hold values from 0 to 2, as said below
- right_root: float32 [8, 64, 6, 128], P('front', 'leaf'), may hold values from -6 to 6
- right_first: float32 [8, 64, 12, 128], P('front', 'leaf'), may hold values from -6 to 6
- right_second: float32 [8, 64, 24, 128], P('front', 'leaf'), may hold values from -6 to 6
- right_third: float32 [8, 64, 48, 128], P('front', 'leaf'), may hold values from -6 to 6
- right_fourth: float32 [8, 64, 96, 128], P('front', 'leaf'), may hold values from -6 to 6
- inverse_root: bfloat16 [3072, 3072], P('leaf', 'front'), as said below
- inverse_first: bfloat16 [6144, 3072], P('leaf', 'front'), as said below
- inverse_second: bfloat16 [12288, 3072], P('leaf', 'front'), as said below
- inverse_third: bfloat16 [24576, 3072], P('leaf', 'front'), as said below
- inverse_fourth: bfloat16 [49152, 3072], P('leaf', 'front'), as said below
- panel_first: bfloat16 [1024, 6144], P('front', 'leaf'), may hold values from -0.0546875 to 0.0546875
- panel_second: bfloat16 [2048, 12288], P('front', 'leaf'), may hold values from -0.0546875 to 0.0546875
- panel_third: bfloat16 [3072, 24576], P('front', 'leaf'), may hold values from -0.0546875 to 0.0546875
- panel_fourth: bfloat16 [4096, 49152], P('front', 'leaf'), may hold values from -0.0546875 to 0.0546875
Outputs:
- answer_root: float32 [8, 64, 6, 128], P('front', 'leaf')
- answer_first: float32 [8, 64, 12, 128], P('front', 'leaf')
- answer_second: float32 [8, 64, 24, 128], P('front', 'leaf')
- answer_third: float32 [8, 64, 48, 128], P('front', 'leaf')
- answer_fourth: float32 [8, 64, 96, 128], P('front', 'leaf')
The draws below stay inside these ranges and needn't reach their ends.
Inputs may be any that keep to these rules, and one draw needn't show every extreme that they name: `added_rows`: entries along the last dimension are distinct. `inverse_root`: each node's inverse is lower triangular with a positive diagonal. `inverse_first`: each node's inverse is lower triangular with a positive diagonal. `inverse_second`: each node's inverse is lower triangular with a positive diagonal. `inverse_third`: each node's inverse is lower triangular with a positive diagonal. `inverse_fourth`: each node's inverse is lower triangular with a positive diagonal.
All inputs are finite; a program needn't handle non-finite values.
Results may differ from the reference program's by a relative error of at most 0.0003.
Values sent between devices are 32-bit elements; how exact they have to be, the bound alone decides.
A program may use at most 64 MiB of HBM per device.

```python
import math
import jax
import jax.numpy as jnp
from jax import lax

B = 128
SB = 24
UBL = 8
R = 128
LEVELS = 5
N_LEAF = 64
N_FRONT = 8


def triangle(key, node_count):
    order_size = SB * B
    lower_part = jax.random.normal(key, (node_count * order_size, order_size), jnp.float32)
    lower_part = jnp.clip(lower_part, -4.0, 4.0) * (0.6 / math.sqrt(order_size))
    diagonal = jax.random.uniform(jax.random.fold_in(key, 7), (node_count * order_size, 1), jnp.float32, 0.75, 1.5)
    row_index = lax.broadcasted_iota(jnp.int32, (node_count * order_size, order_size), 0) % order_size
    col_index = lax.broadcasted_iota(jnp.int32, (node_count * order_size, order_size), 1)
    whole = jnp.where(col_index < row_index, lower_part, jnp.where(col_index == row_index, diagonal, 0.0))
    return whole.astype(jnp.bfloat16)


def draw_inverse_root(key, part):
    return triangle(key, 1)


def draw_inverse_first(key, part):
    return triangle(key, 2)


def draw_inverse_second(key, part):
    return triangle(key, 4)


def draw_inverse_third(key, part):
    return triangle(key, 8)


def draw_inverse_fourth(key, part):
    return triangle(key, 16)


def draw_added_rows(key, part):
    slab_blocks = SB // N_FRONT
    pick_count = UBL // N_FRONT
    shape_all = (2 ** LEVELS - 2, N_FRONT, slab_blocks)
    scores = jax.random.randint(key, shape_all, 0, 1 << 20, jnp.int32) * slab_blocks
    scores = scores + lax.broadcasted_iota(jnp.int32, shape_all, 2)
    return lax.top_k(scores, pick_count)[1].astype(jnp.int32)


def block_levels(rng, shape, cuts, low, largest):
    loudness = 1.0
    for dim, parts in cuts:
        heights = jax.random.uniform(jax.random.fold_in(jax.random.fold_in(rng, 6), dim), (parts,), jnp.float32, low / len(cuts), largest / len(cuts))
        loudness = loudness * jnp.repeat(jnp.exp(heights), shape[dim] // parts).reshape((-1,) + (1,) * (len(shape) - 1 - dim))
    return loudness


def normal_values(stream_key, shape, width, limit, split=(), kind=jnp.bfloat16):
    drawn = jax.random.normal(stream_key, shape, jnp.float32) * width
    if len(split) > 0:
        drawn = block_levels(stream_key, shape, split, -0.22, 0.18) * drawn
    return jnp.clip(drawn, min=-limit, max=limit).astype(kind)


def setup_inputs(seed: int = 0) -> dict:
    streams_of = jax.random.split(jax.random.key(seed), 16)
    added_rows = draw_added_rows(jax.random.fold_in(streams_of[15], 71), 0)
    right_root = normal_values(streams_of[1], (N_FRONT, N_LEAF, SB * B // (N_FRONT * N_LEAF), R), 1.0, 6.0, ((0, 8), (1, 64)), jnp.float32)
    right_first = normal_values(streams_of[2], (N_FRONT, N_LEAF, 2 * SB * B // (N_FRONT * N_LEAF), R), 1.0, 6.0, ((0, 8), (1, 64)), jnp.float32)
    right_second = normal_values(streams_of[3], (N_FRONT, N_LEAF, 4 * SB * B // (N_FRONT * N_LEAF), R), 1.0, 6.0, ((0, 8), (1, 64)), jnp.float32)
    right_third = normal_values(streams_of[4], (N_FRONT, N_LEAF, 8 * SB * B // (N_FRONT * N_LEAF), R), 1.0, 6.0, ((0, 8), (1, 64)), jnp.float32)
    right_fourth = normal_values(streams_of[5], (N_FRONT, N_LEAF, 16 * SB * B // (N_FRONT * N_LEAF), R), 1.0, 6.0, ((0, 8), (1, 64)), jnp.float32)
    inverse_root = draw_inverse_root(jax.random.fold_in(streams_of[15], 71), 0)
    inverse_first = draw_inverse_first(jax.random.fold_in(streams_of[15], 71), 0)
    inverse_second = draw_inverse_second(jax.random.fold_in(streams_of[15], 71), 0)
    inverse_third = draw_inverse_third(jax.random.fold_in(streams_of[15], 71), 0)
    inverse_fourth = draw_inverse_fourth(jax.random.fold_in(streams_of[15], 71), 0)
    panel_first = normal_values(streams_of[11], (UBL * B, 2 * SB * B), (4 * SB * B) ** -0.5, 0.0546875, ((0, 8), (1, 64)))
    panel_second = normal_values(streams_of[12], (2 * UBL * B, 4 * SB * B), (4 * SB * B) ** -0.5, 0.0546875, ((0, 8), (1, 64)))
    panel_third = normal_values(streams_of[13], (3 * UBL * B, 8 * SB * B), (4 * SB * B) ** -0.5, 0.0546875, ((0, 8), (1, 64)))
    panel_fourth = normal_values(streams_of[14], (4 * UBL * B, 16 * SB * B), (4 * SB * B) ** -0.5, 0.0546875, ((0, 8), (1, 64)))
    return {"added_rows": added_rows, "right_root": right_root, "right_first": right_first, "right_second": right_second, "right_third": right_third, "right_fourth": right_fourth, "inverse_root": inverse_root, "inverse_first": inverse_first, "inverse_second": inverse_second, "inverse_third": inverse_third, "inverse_fourth": inverse_fourth, "panel_first": panel_first, "panel_second": panel_second, "panel_third": panel_third, "panel_fourth": panel_fourth}


exact_mode = lax.Precision.HIGHEST


def node_vectors(right_side, level_index):
    node_count = 2 ** level_index
    group_size = N_LEAF // node_count
    shaped = right_side.reshape(N_FRONT, node_count, group_size, right_side.shape[2], right_side.shape[3])
    return jnp.transpose(shaped, (1, 0, 2, 3, 4)).reshape(node_count, SB * B, right_side.shape[3])


def back_layout(values, level_index):
    node_count = 2 ** level_index
    group_size = N_LEAF // node_count
    width_rows = SB * B // (N_FRONT * group_size)
    shaped = values.reshape(node_count, N_FRONT, group_size, width_rows, values.shape[-1])
    return jnp.transpose(shaped, (1, 0, 2, 3, 4)).reshape(N_FRONT, N_LEAF, width_rows, values.shape[-1])


def row_targets(added_rows, level_index):
    node_count = 2 ** level_index
    slab_blocks = SB // N_FRONT
    node_ids = jnp.arange(node_count, dtype=jnp.int32)
    front_ids = jnp.arange(N_FRONT, dtype=jnp.int32)
    targets = []
    for group_index in range(level_index):
        ancestor_level = level_index - 1 - group_index
        holder = node_ids >> (level_index - ancestor_level)
        chooser = node_ids >> (level_index - ancestor_level - 1)
        picked = added_rows[(2 ** (ancestor_level + 1) - 2 + chooser).astype(jnp.int32)]
        blocks = (front_ids[None, :, None] * slab_blocks + picked).astype(jnp.int32)
        targets.append((ancestor_level, holder, blocks))
    return targets


def reference(added_rows, right_root, right_first, right_second, right_third, right_fourth, inverse_root, inverse_first, inverse_second, inverse_third, inverse_fourth, panel_first, panel_second, panel_third, panel_fourth):
    rights = (right_root, right_first, right_second, right_third, right_fourth)
    inverses = (inverse_root, inverse_first, inverse_second, inverse_third, inverse_fourth)
    panels = (None, panel_first, panel_second, panel_third, panel_fourth)
    columns = right_root.shape[3]
    pick_count = UBL // N_FRONT
    order_size = SB * B
    sums = [jnp.zeros((2 ** level_index, SB, B, columns), jnp.float32) for level_index in range(LEVELS)]
    forward = [None] * LEVELS
    for level_index in reversed(range(LEVELS)):
        node_count = 2 ** level_index
        vectors = node_vectors(rights[level_index], level_index)
        inverse = inverses[level_index].astype(jnp.float32).reshape(node_count, order_size, order_size)
        start = vectors - sums[level_index].reshape(node_count, order_size, columns)
        solved = jnp.einsum("nij,njr->nir", inverse, start, precision=exact_mode)
        forward[level_index] = solved
        if level_index > 0:
            panel = panels[level_index].astype(jnp.float32)
            panel_nodes = jnp.transpose(panel.reshape(panel.shape[0], node_count, order_size), (1, 0, 2))
            update = jnp.einsum("nuj,njr->nur", panel_nodes, solved, precision=exact_mode)
            update = update.reshape(node_count, N_FRONT, level_index, pick_count, B, columns)
            for group_index, target in enumerate(row_targets(added_rows, level_index)):
                ancestor_level, holder, blocks = target
                sums[ancestor_level] = sums[ancestor_level].at[holder[:, None, None], blocks].add(update[:, :, group_index])
    solutions = [None] * LEVELS
    answers = []
    for level_index in range(LEVELS):
        node_count = 2 ** level_index
        inverse = inverses[level_index].astype(jnp.float32).reshape(node_count, order_size, order_size)
        target_rows = forward[level_index]
        if level_index > 0:
            panel = panels[level_index].astype(jnp.float32)
            panel_nodes = jnp.transpose(panel.reshape(panel.shape[0], node_count, order_size), (1, 0, 2))
            pieces = []
            for target in row_targets(added_rows, level_index):
                ancestor_level, holder, blocks = target
                pieces.append(solutions[ancestor_level][holder[:, None, None], blocks])
            known = jnp.stack(pieces, axis=2).reshape(node_count, panel.shape[0], columns)
            target_rows = target_rows - jnp.einsum("nuj,nur->njr", panel_nodes, known, precision=exact_mode)
        solved = jnp.einsum("nji,njr->nir", inverse, target_rows, precision=exact_mode)
        solutions[level_index] = solved.reshape(node_count, SB, B, columns)
        answers.append(back_layout(solved, level_index))
    return (answers[0], answers[1], answers[2], answers[3], answers[4])
```

```python
import jax
import jax.numpy as jnp
from jax import lax
from jax.experimental import pallas as pl
from jax.experimental.pallas import tpu as pltpu
from jax.sharding import PartitionSpec as P

MESH = pl.DeviceIdType.MESH
B = 128
LEVELS = 5
NZ = 16
NX = 4
NY = 4
SLAB = 384
ROWS = (48, 96, 192, 384, 768)
OWN = (6, 12, 24, 48, 96)

SCRATCH = {
    "bx0": (4, 6, 128), "bx1": (2, 12, 128),
    "b0": (16, 4, 6, 128), "b1": (16, 2, 12, 128), "b2": (SLAB, 128), "b3": (SLAB, 128), "c4": (SLAB, 128),
    "c3": (SLAB, 128), "c2": (SLAB, 128), "c1": (SLAB, 128), "c0": (SLAB, 128),
    "u4": (512, 128), "u3": (384, 128), "u2": (256, 128), "u1": (128, 128),
    "ur4": (4, 32, 128), "us4": (32, 128), "ug4": (256, 128),
    "ur3": (8, 16, 128), "us3": (16, 128), "ug3": (256, 128),
    "ur2": (16, 8, 128), "us2": (2, 8, 128), "ug2": (16, 2, 8, 128),
    "ur1": (16, 8, 128), "ux1": (4, 8, 128), "uo1": (8, 128), "us1": (2, 8, 128), "ug1": (16, 2, 8, 128),
    "s0": (SLAB, 128), "s1": (SLAB, 128), "s2": (SLAB, 128), "s3": (SLAB, 128), "s4": (SLAB, 128),
    "k0": (16, 2, 8, 128), "kr0": (16, 2, 8, 128), "kx0": (2, 8, 128), "kt0": (4, 8, 128), "ks0": (8, 128), "z0": (16, 8, 128),
    "k1": (16, 2, 8, 128), "kr1": (16, 2, 8, 128), "kx1": (2, 8, 128), "kt1": (8, 128), "ks1": (8, 128), "z1": (16, 8, 128),
    "k2": (256, 128), "kr2": (16, 16, 128), "ks2": (16, 128), "z2": (128, 128),
    "k3": (256, 128), "kr3": (8, 32, 128), "ks3": (32, 128), "z3": (128, 128),
    "ar4": (4, 96, 128), "ar3": (8, 48, 128), "ar2": (16, 24, 128),
    "ax1": (192, 128), "am1": (192, 128), "ap1": (16, 12, 128), "ar1": (16, 12, 128),
    "ax0": (4, 96, 128), "am0": (96, 128), "ap0": (16, 6, 128), "ar0": (16, 6, 128),
}
for _way in "fb":
    for _l in range(LEVELS):
        _h = ROWS[_l] // 2
        SCRATCH[f"{_way}p{_l}"] = (2 * _h, 128)
        SCRATCH[f"{_way}c{_l}"] = (_h, 128)
        SCRATCH[f"{_way}h{_l}"] = (_h, 128)
        if _l >= 3:
            SCRATCH[f"{_way}r{_l}"] = (4, _h // 4, 128)
            SCRATCH[f"{_way}q{_l}"] = (_h // 4, 128)
            SCRATCH[f"{_way}g{_l}"] = (_h, 128)
        else:
            SCRATCH[f"{_way}r{_l}"] = (4, _h, 128)
            SCRATCH[f"{_way}g{_l}"] = (_h, 128)
        SCRATCH[f"{_way}y{_l}"] = (2 * _h, 128)
NAMES = tuple(SCRATCH)
SEMS = 128


def split(values):
    high = values.astype(jnp.bfloat16)
    low = (values - high.astype(jnp.float32)).astype(jnp.bfloat16)
    return jnp.concatenate([high, low], axis=1)


def times(matrix, values):
    both = jnp.dot(matrix, split(values), preferred_element_type=jnp.float32)
    return both[:, :128] + both[:, 128:]


def transposed_times(matrix, values):
    both = lax.dot_general(
        matrix, split(values), (((0,), (0,)), ((), ())), preferred_element_type=jnp.float32
    )
    return both[:, :128] + both[:, 128:]


def rows_of(index, count):
    return pl.ds(pl.multiple_of(index * count, 8), count)


def total(ref):
    parts = [ref[j] for j in range(ref.shape[0])]
    while len(parts) > 1:
        parts = [parts[j] + parts[j + 1] for j in range(0, len(parts), 2)]
    return parts[0]


def kernel(added, *refs):
    rights, refs = refs[:5], refs[5:]
    inverses, refs = refs[:5], refs[5:]
    panels, refs = (None,) + refs[:4], refs[4:]
    outs, refs = refs[:5], refs[5:]
    v = dict(zip(NAMES, refs[: len(NAMES)]))
    send_sems, recv_sems = refs[len(NAMES) :]

    leaf = lax.axis_index("leaf")
    front = lax.axis_index("front")
    x, z = leaf // NZ, leaf % NZ
    y, core = front // 2, front % 2
    pair = x % 2

    counter = [0]
    sent = []

    def at_z(n, i):
        d = n // 2 + (i + 1) // 2 * (1 - 2 * (i % 2))
        there = (z % n + d) % n
        return there, (x * NZ + z - z % n + there, front)

    def at_x(d):
        other = (x + d) % NX
        return other, (other * NZ + z, front)

    x_mate = ((x + 1 - 2 * pair) * NZ + z, front)
    core_mate = (leaf, front + 1 - 2 * core)

    def at_y(d):
        other = (y + d) % NY
        return other, (leaf, other * 2 + core)

    def begin():
        counter[0] += 1
        return counter[0] - 1

    def send(src, dst, k, device):
        pltpu.make_async_remote_copy(
            src_ref=src, dst_ref=dst, send_sem=send_sems.at[k], recv_sem=recv_sems.at[k],
            device_id=device, device_id_type=MESH,
        ).start()

    def await_bytes(like, k, sems):
        pltpu.make_async_copy(like, like, sems.at[k]).wait()

    def scatter_z(n, src, rows, dst):
        k = begin()
        whole_pieces = len(src.shape) > 2

        def piece(i):
            return src.at[i] if whole_pieces else src.at[rows_of(i, rows)]

        def step(i, _):
            there, device = at_z(n, i)
            send(piece(there), dst.at[z % n], k, device)
            return 0

        lax.fori_loop(0, n - 1, step, 0)
        here = z % n
        dst[here] = src[here] if whole_pieces else src[rows_of(here, rows), :]
        like = dst.at[pl.ds(0, n - 1)]
        sent.append((like, k))
        return lambda: await_bytes(like, k, recv_sems)

    def gather_z(n, src, rows, dst):
        k = begin()
        whole_pieces = len(dst.shape) > 2
        here = z % n
        spot = dst.at[here] if whole_pieces else dst.at[rows_of(here, rows)]

        def step(i, _):
            _, device = at_z(n, i)
            send(src, spot, k, device)
            return 0

        lax.fori_loop(0, n - 1, step, 0)
        if whole_pieces:
            dst[here] = src[...]
        else:
            dst[rows_of(here, rows), :] = src[...]
        like = dst.at[pl.ds(0, (n - 1) if whole_pieces else (n - 1) * rows)]
        sent.append((like, k))
        return lambda: await_bytes(like, k, recv_sems)

    def to_one(src, dst, device):
        k = begin()
        send(src, dst, k, device)
        sent.append((dst, k))
        return lambda: await_bytes(dst, k, recv_sems)

    def to_x(pieces, dst):
        k = begin()
        for d in (2, 1, 3):
            other, device = at_x(d)
            send(pieces(other), dst.at[x], k, device)
        like = dst.at[pl.ds(0, 3)]
        sent.append((like, k))
        return lambda: await_bytes(like, k, recv_sems)

    def to_y(pieces, spot, like):
        k = begin()
        for d in (2, 1, 3):
            other, device = at_y(d)
            send(pieces(other), spot, k, device)
        sent.append((like, k))
        return lambda: await_bytes(like, k, recv_sems)

    def front_sum(way, level, meanwhile=None):
        term, from_core, half = v[f"{way}p{level}"], v[f"{way}c{level}"], v[f"{way}h{level}"]
        received, summed, whole = v[f"{way}r{level}"], v[f"{way}g{level}"], v[f"{way}y{level}"]
        h = ROWS[level] // 2
        done = to_one(term.at[rows_of(1 - core, h)], from_core, core_mate)
        done()
        half[...] = term[rows_of(core, h), :] + from_core[...]
        if level >= 3:
            q = h // 4
            piece = v[f"{way}q{level}"]
            done = to_y(lambda other: half.at[rows_of(other, q)], received.at[y], received.at[pl.ds(0, 3)])
            received[y] = half[rows_of(y, q), :]
            if meanwhile is not None:
                meanwhile()
            done()
            piece[...] = total(received)
            done = to_y(lambda other: piece, summed.at[rows_of(y, q)], summed.at[pl.ds(0, 3 * q)])
            summed[rows_of(y, q), :] = piece[...]
            done()
        else:
            done = to_y(lambda other: half, received.at[y], received.at[pl.ds(0, 3)])
            received[y] = half[...]
            if meanwhile is not None:
                meanwhile()
            done()
            summed[...] = total(received)
        done = to_one(summed, whole.at[rows_of(core, h)], core_mate)
        whole[rows_of(core, h), :] = summed[...]
        done()
        return whole

    def choice(level, child):
        block = added[2 ** (level + 1) - 2 + child, front, 0]
        return [jnp.where(block == j, 1.0, 0.0).astype(jnp.float32) for j in range(3)]

    def choices(level):
        node = leaf // (64 >> level)
        return choice(level, 2 * node), choice(level, 2 * node + 1)

    def place(level, b, low, high):
        to_low, to_high = choices(level)
        target = v[f"c{level}"]
        for j in range(3):
            spot = slice(j * B, (j + 1) * B)
            target[spot, :] = b[spot, :] - low * to_low[j] - high * to_high[j]

    def pick(s, weights):
        return s[0:B, :] * weights[0] + s[B : 2 * B, :] * weights[1] + s[2 * B :, :] * weights[2]

    barrier = pltpu.get_barrier_semaphore()

    def greet(i, _):
        _, device = at_z(NZ, i)
        pl.semaphore_signal(barrier, inc=1, device_id=device, device_id_type=MESH)
        return 0

    lax.fori_loop(0, NZ - 1, greet, 0)
    for d in (1, 2, 3):
        pl.semaphore_signal(barrier, inc=1, device_id=at_x(d)[1], device_id_type=MESH)
        pl.semaphore_signal(barrier, inc=1, device_id=at_y(d)[1], device_id_type=MESH)
    pl.semaphore_signal(barrier, inc=1, device_id=core_mate, device_id_type=MESH)
    pl.semaphore_wait(barrier, NZ - 1 + 7)

    done_b4 = gather_z(4, rights[4].at[0, 0], 96, v["c4"])
    done_b3 = gather_z(8, rights[3].at[0, 0], 48, v["b3"])
    done_x1 = to_one(rights[1].at[0, 0], v["bx1"].at[pair], x_mate)
    v["bx1"][pair] = rights[1][0, 0]
    done_x0 = to_x(lambda other: rights[0].at[0, 0], v["bx0"])
    v["bx0"][x] = rights[0][0, 0]
    done_b = {}

    def more_b2():
        done_b[2] = gather_z(NZ, rights[2].at[0, 0], 24, v["b2"])

    def more_b1():
        done_x1()
        done_x0()
        done_b[1] = gather_z(NZ, v["bx1"], 24, v["b1"])
        done_b[0] = gather_z(NZ, v["bx0"], 24, v["b0"])

    done_b4()
    v["fp4"][...] = times(inverses[4][...], v["c4"][...])
    y4 = front_sum("f", 4, more_b2)
    v["u4"][...] = times(panels[4][...], y4[...])
    scatter_z(4, v["u4"], 32, v["ur4"])()
    v["us4"][...] = total(v["ur4"])
    done = gather_z(8, v["us4"], 32, v["ug4"])
    done_b3()
    done()

    place(3, v["b3"], v["ug4"][0:B, :], v["ug4"][B:, :])
    v["fp3"][...] = times(inverses[3][...], v["c3"][...])
    y3 = front_sum("f", 3, more_b1)
    v["u3"][...] = times(panels[3][...], y3[...]) + v["u4"][B:, :]
    scatter_z(8, v["u3"], 16, v["ur3"])()
    v["us3"][...] = total(v["ur3"])
    done = gather_z(NZ, v["us3"], 16, v["ug3"])
    done_b[2]()
    done()

    place(2, v["b2"], v["ug3"][0:B, :], v["ug3"][B:, :])
    v["fp2"][...] = times(inverses[2][...], v["c2"][...])
    y2 = front_sum("f", 2)
    v["u2"][...] = times(panels[2][...], y2[...]) + v["u3"][B:, :]
    scatter_z(NZ, v["u2"], 8, v["ur2"])()
    v["us2"][pair] = total(v["ur2"])
    to_one(v["us2"].at[pair], v["us2"].at[pair], x_mate)()
    done = gather_z(NZ, v["us2"], 16, v["ug2"])
    done_b[1]()
    for p in range(32):
        v["c1"][12 * p : 12 * p + 12, :] = v["b1"][p % 16, p // 16]
    done()

    low, high = (v["ug2"][:, j].reshape(B, 128) for j in range(2))
    place(1, v["c1"], low, high)
    v["fp1"][...] = times(inverses[1][...], v["c1"][...])
    y1 = front_sum("f", 1)
    v["u1"][...] = times(panels[1][...], y1[...]) + v["u2"][B:, :]
    scatter_z(NZ, v["u1"], 8, v["ur1"])()
    own = total(v["ur1"])
    v["uo1"][...] = own
    v["ux1"][x] = own
    to_x(lambda other: v["uo1"], v["ux1"])()
    v["us1"][0] = v["ux1"][0] + v["ux1"][1]
    v["us1"][1] = v["ux1"][2] + v["ux1"][3]
    done = gather_z(NZ, v["us1"], 16, v["ug1"])
    done_b[0]()
    for p in range(64):
        v["c0"][6 * p : 6 * p + 6, :] = v["b0"][p % 16, p // 16]
    done()

    low, high = (v["ug1"][:, j].reshape(B, 128) for j in range(2))
    place(0, v["c0"], low, high)
    v["fp0"][...] = times(inverses[0][...], v["c0"][...])
    y0 = front_sum("f", 0)

    def solve(level, right_side):
        v[f"s{level}"][...] = transposed_times(inverses[level][...], right_side)

    def picked(level):
        to_low, to_high = choices(level)
        s = v[f"s{level}"]
        return pick(s, to_low), pick(s, to_high)

    def remove(level, known, meanwhile=None):
        v[f"bp{level}"][...] = transposed_times(panels[level][...], known)
        through = front_sum("b", level, meanwhile)
        return v[f"fy{level}"][...] - through[...]

    answers = {}
    solve(0, y0[...])
    for j, rows in enumerate(picked(0)):
        v["k0"][:, j] = rows.reshape(16, 8, 128)
    scatter_z(NZ, v["k0"], 8, v["kr0"])()
    v["kx0"][...] = total(v["kr0"])
    done = to_x(lambda other: v["kx0"].at[other // 2], v["kt0"])
    v["kt0"][x] = v["kx0"][x // 2]
    done()
    v["ks0"][...] = total(v["kt0"])
    done = gather_z(NZ, v["ks0"], 8, v["z0"])
    done_a0 = to_x(lambda other: v["s0"].at[rows_of(other, 96)], v["ax0"])
    v["ax0"][x] = v["s0"][rows_of(x, 96), :]
    done()
    known = v["z0"][...].reshape(B, 128)

    def root_answer():
        done_a0()
        v["am0"][...] = total(v["ax0"])
        for p in range(16):
            v["ap0"][p] = v["am0"][6 * p : 6 * p + 6, :]
        answers[0] = scatter_z(NZ, v["ap0"], 6, v["ar0"])

    solve(1, remove(1, known, root_answer))
    for j, rows in enumerate(picked(1)):
        v["k1"][:, j] = rows.reshape(16, 8, 128)
    scatter_z(NZ, v["k1"], 8, v["kr1"])()
    v["kx1"][...] = total(v["kr1"])
    to_one(v["kx1"].at[1 - pair], v["kt1"], x_mate)()
    v["ks1"][...] = v["kx1"][pair] + v["kt1"][...]
    done = gather_z(NZ, v["ks1"], 8, v["z1"])
    done_a1 = to_one(v["s1"].at[rows_of(1 - pair, 192)], v["ax1"], x_mate)
    done()
    known = jnp.concatenate([v["z1"][...].reshape(B, 128), known], 0)

    def first_answer():
        done_a1()
        v["am1"][...] = v["s1"][rows_of(pair, 192), :] + v["ax1"][...]
        for p in range(16):
            v["ap1"][p] = v["am1"][12 * p : 12 * p + 12, :]
        answers[1] = scatter_z(NZ, v["ap1"], 12, v["ar1"])

    solve(2, remove(2, known, first_answer))
    for j, rows in enumerate(picked(2)):
        v["k2"][j * B : (j + 1) * B, :] = rows
    scatter_z(NZ, v["k2"], 16, v["kr2"])()
    v["ks2"][...] = total(v["kr2"])
    gather_z(8, v["ks2"], 16, v["z2"])()
    known = jnp.concatenate([v["z2"][...], known], 0)

    def second_answer():
        answers[2] = scatter_z(NZ, v["s2"], 24, v["ar2"])

    solve(3, remove(3, known, second_answer))
    for j, rows in enumerate(picked(3)):
        v["k3"][j * B : (j + 1) * B, :] = rows
    scatter_z(8, v["k3"], 32, v["kr3"])()
    v["ks3"][...] = total(v["kr3"])
    gather_z(4, v["ks3"], 32, v["z3"])()
    known = jnp.concatenate([v["z3"][...], known], 0)

    def third_answer():
        answers[3] = scatter_z(8, v["s3"], 48, v["ar3"])

    solve(4, remove(4, known, third_answer))
    answers[4] = scatter_z(4, v["s4"], 96, v["ar4"])
    for level in range(LEVELS):
        answers[level]()
        outs[level][0, 0] = total(v[f"ar{level}"])
    for like, k in sent:
        await_bytes(like, k, send_sems)


def per_device(added_rows, *arrays):
    vmem = pl.BlockSpec(memory_space=pltpu.VMEM)
    return pl.pallas_call(
        kernel,
        out_shape=tuple(jax.ShapeDtypeStruct((1, 1, w, 128), jnp.float32) for w in OWN),
        in_specs=[pl.BlockSpec(memory_space=pltpu.SMEM)] + [vmem] * 14,
        out_specs=(vmem,) * 5,
        scratch_shapes=[pltpu.VMEM(shape, jnp.float32) for shape in SCRATCH.values()]
        + [pltpu.SemaphoreType.DMA((SEMS,)), pltpu.SemaphoreType.DMA((SEMS,))],
        compiler_params=pltpu.CompilerParams(
            collective_id=0, has_side_effects=True, vmem_limit_bytes=48 * 2**20
        ),
        cost_estimate=pl.CostEstimate(flops=1_200_000_000, bytes_accessed=3_000_000, transcendentals=0),
        name="solve",
    )(added_rows, *arrays)


def solution(mesh):
    rights, inverses, panels = P("front", "leaf", None, None), P("leaf", "front"), P("front", "leaf")
    return jax.shard_map(
        per_device,
        mesh=mesh,
        in_specs=(P(),) + (rights,) * 5 + (inverses,) * 5 + (panels,) * 4,
        out_specs=(rights,) * 5,
        check_vma=False,
    )
```

```python
import jax
import jax.numpy as jnp
from jax import lax
from jax.experimental import pallas as pl
from jax.experimental.pallas import tpu as pltpu
from jax.sharding import PartitionSpec as P

MESH = pl.DeviceIdType.MESH
B = 128
LEVELS = 5
NZ = 16
NX = 4
NY = 4
SLAB = 384
ROWS = (48, 96, 192, 384, 768)
OWN = (6, 12, 24, 48, 96)

SCRATCH = {
    "bx0": (4, 6, 128), "bx1": (2, 12, 128),
    "b0": (16, 4, 6, 128), "b1": (16, 2, 12, 128), "b2": (SLAB, 128), "b3": (SLAB, 128), "c4": (SLAB, 128),
    "c3": (SLAB, 128), "c2": (SLAB, 128), "c1": (SLAB, 128), "c0": (SLAB, 128),
    "u4": (512, 128), "u3": (384, 128), "u2": (256, 128), "u1": (128, 128),
    "ur4": (4, 32, 128), "us4": (32, 128), "ug4": (256, 128),
    "ur3": (8, 16, 128), "us3": (16, 128), "ug3": (256, 128),
    "ur2": (16, 8, 128), "us2": (2, 8, 128), "ug2": (16, 2, 8, 128),
    "ur1": (16, 8, 128), "ux1": (4, 8, 128), "uo1": (8, 128), "us1": (2, 8, 128), "ug1": (16, 2, 8, 128),
    "s0": (SLAB, 128), "s1": (SLAB, 128), "s2": (SLAB, 128), "s3": (SLAB, 128), "s4": (SLAB, 128),
    "k0": (16, 2, 8, 128), "kr0": (16, 2, 8, 128), "kx0": (2, 8, 128), "kt0": (4, 8, 128), "ks0": (8, 128), "z0": (16, 8, 128),
    "k1": (16, 2, 8, 128), "kr1": (16, 2, 8, 128), "kx1": (2, 8, 128), "kt1": (8, 128), "ks1": (8, 128), "z1": (16, 8, 128),
    "k2": (256, 128), "kr2": (16, 16, 128), "ks2": (16, 128), "z2": (128, 128),
    "k3": (256, 128), "kr3": (8, 32, 128), "ks3": (32, 128), "z3": (128, 128),
    "ar4": (4, 96, 128), "ar3": (8, 48, 128), "ar2": (16, 24, 128),
    "ax1": (192, 128), "am1": (192, 128), "ap1": (16, 12, 128), "ar1": (16, 12, 128),
    "ax0": (4, 96, 128), "am0": (96, 128), "ap0": (16, 6, 128), "ar0": (16, 6, 128),
}
for _way in "fb":
    for _l in range(LEVELS):
        _h = ROWS[_l] // 2
        SCRATCH[f"{_way}p{_l}"] = (2 * _h, 128)
        SCRATCH[f"{_way}c{_l}"] = (_h, 128)
        SCRATCH[f"{_way}h{_l}"] = (_h, 128)
        if _l < 2:
            SCRATCH[f"{_way}r{_l}"] = (4, 2 * _h, 128)
            SCRATCH[f"{_way}h{_l}"] = (2 * _h, 128)
            SCRATCH[f"{_way}g{_l}"] = (2 * _h, 128)
        elif _l >= 3:
            SCRATCH[f"{_way}r{_l}"] = (4, _h // 4, 128)
            SCRATCH[f"{_way}q{_l}"] = (_h // 4, 128)
            SCRATCH[f"{_way}g{_l}"] = (_h, 128)
        else:
            SCRATCH[f"{_way}r{_l}"] = (4, _h, 128)
            SCRATCH[f"{_way}g{_l}"] = (_h, 128)
        SCRATCH[f"{_way}y{_l}"] = (2 * _h, 128)
NAMES = tuple(SCRATCH)
SEMS = 128
MATRICES = {
    "g0": (48, 384), "g1": (96, 384), "g2": (192, 384), "g3": (384, 384), "g4": (768, 384),
    "q1": (96, 128), "q2": (192, 256), "p3": (384, 384), "p4": (512, 768),
    "h0": (384, 48), "h1": (384, 96), "h2": (384, 192), "h3": (384, 384), "h4": (384, 768),
    "p1": (128, 96), "p2": (256, 192), "q3": (384, 384), "q4": (768, 512),
}
LOADED = tuple(MATRICES)[:9]


def split(values):
    high = values.astype(jnp.bfloat16)
    low = (values - high.astype(jnp.float32)).astype(jnp.bfloat16)
    return jnp.concatenate([high, low], axis=1)


def times(matrix, values):
    both = jnp.dot(matrix, split(values), preferred_element_type=jnp.float32)
    return both[:, :128] + both[:, 128:]


def rows_of(index, count):
    return pl.ds(pl.multiple_of(index * count, 8), count)


def total(ref):
    parts = [ref[j] for j in range(ref.shape[0])]
    while len(parts) > 1:
        parts = [parts[j] + parts[j + 1] for j in range(0, len(parts), 2)]
    return parts[0]


def kernel(added, *refs):
    stored_rights, refs = refs[:5], refs[5:]
    stored, refs = refs[:9], refs[9:]
    outs, refs = refs[:5], refs[5:]
    v = dict(zip(NAMES, refs[: len(NAMES)]))
    refs = refs[len(NAMES) :]
    m = dict(zip(MATRICES, refs[: len(MATRICES)]))
    rights, refs = refs[len(MATRICES) : len(MATRICES) + 5], refs[len(MATRICES) + 5 :]
    send_sems, recv_sems, load_sems = refs

    leaf = lax.axis_index("leaf")
    front = lax.axis_index("front")
    x, z = leaf // NZ, leaf % NZ
    y, core = front // 2, front % 2
    pair = x % 2

    counter = [0]
    sent = []

    def at_z(n, i):
        d = n // 2 + (i + 1) // 2 * (1 - 2 * (i % 2))
        there = (z % n + d) % n
        return there, (x * NZ + z - z % n + there, front)

    def at_x(d):
        other = (x + d) % NX
        return other, (other * NZ + z, front)

    x_mate = ((x + 1 - 2 * pair) * NZ + z, front)
    core_mate = (leaf, front + 1 - 2 * core)

    def at_y(d):
        other = (y + d) % NY
        return other, (leaf, other * 2 + core)

    def begin():
        counter[0] += 1
        return counter[0] - 1

    def send(src, dst, k, device):
        pltpu.make_async_remote_copy(
            src_ref=src, dst_ref=dst, send_sem=send_sems.at[k], recv_sem=recv_sems.at[k],
            device_id=device, device_id_type=MESH,
        ).start()

    def await_bytes(like, k, sems):
        pltpu.make_async_copy(like, like, sems.at[k]).wait()

    def scatter_z(n, src, rows, dst):
        k = begin()
        whole_pieces = len(src.shape) > 2

        def piece(i):
            return src.at[i] if whole_pieces else src.at[rows_of(i, rows)]

        def step(i, _):
            there, device = at_z(n, i)
            send(piece(there), dst.at[z % n], k, device)
            return 0

        lax.fori_loop(0, n - 1, step, 0)
        here = z % n
        dst[here] = src[here] if whole_pieces else src[rows_of(here, rows), :]
        like = dst.at[pl.ds(0, n - 1)]
        sent.append((like, k))
        return lambda: await_bytes(like, k, recv_sems)

    def gather_z(n, src, rows, dst):
        k = begin()
        whole_pieces = len(dst.shape) > 2
        here = z % n
        spot = dst.at[here] if whole_pieces else dst.at[rows_of(here, rows)]

        def step(i, _):
            _, device = at_z(n, i)
            send(src, spot, k, device)
            return 0

        lax.fori_loop(0, n - 1, step, 0)
        if whole_pieces:
            dst[here] = src[...]
        else:
            dst[rows_of(here, rows), :] = src[...]
        like = dst.at[pl.ds(0, (n - 1) if whole_pieces else (n - 1) * rows)]
        sent.append((like, k))
        return lambda: await_bytes(like, k, recv_sems)

    def to_one(src, dst, device):
        k = begin()
        send(src, dst, k, device)
        sent.append((dst, k))
        return lambda: await_bytes(dst, k, recv_sems)

    def to_x(pieces, dst):
        k = begin()
        for d in (2, 1, 3):
            other, device = at_x(d)
            send(pieces(other), dst.at[x], k, device)
        like = dst.at[pl.ds(0, 3)]
        sent.append((like, k))
        return lambda: await_bytes(like, k, recv_sems)

    def to_y(pieces, spot, like):
        k = begin()
        for d in (2, 1, 3):
            other, device = at_y(d)
            send(pieces(other), spot, k, device)
        sent.append((like, k))
        return lambda: await_bytes(like, k, recv_sems)

    def front_sum(way, level, meanwhile=None):
        term, half, whole = v[f"{way}p{level}"], v[f"{way}h{level}"], v[f"{way}y{level}"]
        received, summed = v[f"{way}r{level}"], v[f"{way}g{level}"]
        if level < 2:
            done = to_y(lambda other: term, received.at[y], received.at[pl.ds(0, 3)])
            received[y] = term[...]
            if meanwhile is not None:
                meanwhile()
            done()
            half[...] = total(received)
            done = to_one(half, summed, core_mate)
            done()
            whole[...] = half[...] + summed[...]
            return whole
        h = ROWS[level] // 2
        from_core = v[f"{way}c{level}"]
        done = to_one(term.at[rows_of(1 - core, h)], from_core, core_mate)
        done()
        half[...] = term[rows_of(core, h), :] + from_core[...]
        if level >= 3:
            q = h // 4
            piece = v[f"{way}q{level}"]
            done = to_y(lambda other: half.at[rows_of(other, q)], received.at[y], received.at[pl.ds(0, 3)])
            received[y] = half[rows_of(y, q), :]
            if meanwhile is not None:
                meanwhile()
            done()
            piece[...] = total(received)
            done = to_y(lambda other: piece, summed.at[rows_of(y, q)], summed.at[pl.ds(0, 3 * q)])
            summed[rows_of(y, q), :] = piece[...]
            done()
        else:
            done = to_y(lambda other: half, received.at[y], received.at[pl.ds(0, 3)])
            received[y] = half[...]
            if meanwhile is not None:
                meanwhile()
            done()
            summed[...] = total(received)
        done = to_one(summed, whole.at[rows_of(core, h)], core_mate)
        whole[rows_of(core, h), :] = summed[...]
        done()
        return whole

    def choice(level, child):
        block = added[front, 0, 2 ** (level + 1) - 2 + child]
        return [jnp.where(block == j, 1.0, 0.0).astype(jnp.float32) for j in range(3)]

    def choices(level):
        node = leaf // (64 >> level)
        return choice(level, 2 * node), choice(level, 2 * node + 1)

    def place(level, b, low, high):
        to_low, to_high = choices(level)
        target = v[f"c{level}"]
        for j in range(3):
            spot = slice(j * B, (j + 1) * B)
            target[spot, :] = b[spot, :] - low * to_low[j] - high * to_high[j]

    def pick(s, weights):
        return s[0:B, :] * weights[0] + s[B : 2 * B, :] * weights[1] + s[2 * B :, :] * weights[2]

    loads = {}

    def load(name, src, dst, k):
        copy = pltpu.make_async_copy(src, dst, load_sems.at[k])
        copy.start()
        loads[name] = copy.wait

    load("r4", stored_rights[4].at[0, 0], rights[4], 4)
    load("g4", stored[4], m["g4"], 9)
    for level in (3, 2):
        load(f"r{level}", stored_rights[level].at[0, 0], rights[level], level)
    for level in (1, 0):
        for i in range(OWN[level]):
            pltpu.make_async_copy(
                stored_rights[level].at[0, i], rights[level].at[pl.ds(i, 1)], load_sems.at[level]
            ).start()
    for k, name in enumerate(LOADED):
        if name != "g4":
            load(name, stored[k], m[name], 5 + k)

    barrier = pltpu.get_barrier_semaphore()

    def greet(device):
        pl.semaphore_signal(barrier, inc=1, device_id=device, device_id_type=MESH)

    greet((x * NZ + (z + 4) % NZ, front))
    greet((x * NZ + (z + 12) % NZ, front))
    for i in range(3):
        greet(at_z(4, i)[1])
    for d in (1, 2, 3):
        greet(at_x(d)[1])
        greet(at_y(d)[1])
    greet(core_mate)
    pl.semaphore_wait(barrier, 12)

    loads["r4"]()
    done_b4 = gather_z(4, rights[4], 96, v["c4"])
    await_bytes(rights[1], 1, load_sems)
    done_x1 = to_one(rights[1], v["bx1"].at[pair], x_mate)
    v["bx1"][pair] = rights[1][...]
    await_bytes(rights[0], 0, load_sems)
    done_x0 = to_x(lambda other: rights[0], v["bx0"])
    v["bx0"][x] = rights[0][...]
    for name in ("r3", "r2") + LOADED:
        loads[name]()
    done_b = {}

    def turn(*names):
        for source, target in names:
            m[target][...] = m[source][...].T

    def more_b3():
        done_b[3] = gather_z(8, rights[3], 48, v["b3"])

    def more_b2():
        done_b[2] = gather_z(NZ, rights[2], 24, v["b2"])

    def more_b1():
        done_x1()
        done_b[1] = gather_z(NZ, v["bx1"], 24, v["b1"])

    def more_b0():
        done_x0()
        done_b[0] = gather_z(NZ, v["bx0"], 24, v["b0"])

    turn(("g4", "h4"))
    done_b4()
    v["fp4"][...] = times(m["g4"][...], v["c4"][...])
    y4 = front_sum("f", 4, more_b3)
    v["u4"][...] = times(m["p4"][...], y4[...])
    done = scatter_z(4, v["u4"], 32, v["ur4"])
    turn(("p4", "q4"))
    done()
    v["us4"][...] = total(v["ur4"])
    done = gather_z(8, v["us4"], 32, v["ug4"])
    turn(("g3", "h3"), ("q2", "p2"), ("q1", "p1"))
    done_b[3]()
    done()

    place(3, v["b3"], v["ug4"][0:B, :], v["ug4"][B:, :])
    v["fp3"][...] = times(m["g3"][...], v["c3"][...])
    y3 = front_sum("f", 3, more_b2)
    v["u3"][...] = times(m["p3"][...], y3[...]) + v["u4"][B:, :]
    done = scatter_z(8, v["u3"], 16, v["ur3"])
    turn(("p3", "q3"))
    done()
    v["us3"][...] = total(v["ur3"])
    done = gather_z(NZ, v["us3"], 16, v["ug3"])
    turn(("g2", "h2"), ("g1", "h1"), ("g0", "h0"))
    done_b[2]()
    done()

    place(2, v["b2"], v["ug3"][0:B, :], v["ug3"][B:, :])
    v["fp2"][...] = times(m["g2"][...], v["c2"][...])
    y2 = front_sum("f", 2, more_b1)
    v["u2"][...] = times(m["p2"][...], y2[...]) + v["u3"][B:, :]
    scatter_z(NZ, v["u2"], 8, v["ur2"])()
    v["us2"][pair] = total(v["ur2"])
    to_one(v["us2"].at[pair], v["us2"].at[pair], x_mate)()
    done = gather_z(NZ, v["us2"], 16, v["ug2"])
    done_b[1]()
    for p in range(32):
        v["c1"][12 * p : 12 * p + 12, :] = v["b1"][p % 16, p // 16]
    done()

    low, high = (v["ug2"][:, j].reshape(B, 128) for j in range(2))
    place(1, v["c1"], low, high)
    v["fp1"][...] = times(m["g1"][...], v["c1"][...])
    y1 = front_sum("f", 1, more_b0)
    v["u1"][...] = times(m["p1"][...], y1[...]) + v["u2"][B:, :]
    scatter_z(NZ, v["u1"], 8, v["ur1"])()
    own = total(v["ur1"])
    v["uo1"][...] = own
    v["ux1"][x] = own
    to_x(lambda other: v["uo1"], v["ux1"])()
    v["us1"][0] = v["ux1"][0] + v["ux1"][1]
    v["us1"][1] = v["ux1"][2] + v["ux1"][3]
    done = gather_z(NZ, v["us1"], 16, v["ug1"])
    done_b[0]()
    for p in range(64):
        v["c0"][6 * p : 6 * p + 6, :] = v["b0"][p % 16, p // 16]
    done()

    low, high = (v["ug1"][:, j].reshape(B, 128) for j in range(2))
    place(0, v["c0"], low, high)
    v["fp0"][...] = times(m["g0"][...], v["c0"][...])
    y0 = front_sum("f", 0)

    def solve(level, right_side):
        v[f"s{level}"][...] = times(m[f"h{level}"][...], right_side)

    def picked(level):
        to_low, to_high = choices(level)
        s = v[f"s{level}"]
        return pick(s, to_low), pick(s, to_high)

    def remove(level, known, meanwhile=None):
        v[f"bp{level}"][...] = times(m[f"q{level}"][...], known)
        through = front_sum("b", level, meanwhile)
        return v[f"fy{level}"][...] - through[...]

    answers = {}
    solve(0, y0[...])
    for j, rows in enumerate(picked(0)):
        v["k0"][:, j] = rows.reshape(16, 8, 128)
    scatter_z(NZ, v["k0"], 8, v["kr0"])()
    v["kx0"][...] = total(v["kr0"])
    done = to_x(lambda other: v["kx0"].at[other // 2], v["kt0"])
    v["kt0"][x] = v["kx0"][x // 2]
    done()
    v["ks0"][...] = total(v["kt0"])
    done = gather_z(NZ, v["ks0"], 8, v["z0"])
    done_a0 = to_x(lambda other: v["s0"].at[rows_of(other, 96)], v["ax0"])
    v["ax0"][x] = v["s0"][rows_of(x, 96), :]
    done()
    known = v["z0"][...].reshape(B, 128)

    def root_answer():
        done_a0()
        v["am0"][...] = total(v["ax0"])
        for p in range(16):
            v["ap0"][p] = v["am0"][6 * p : 6 * p + 6, :]
        answers[0] = scatter_z(NZ, v["ap0"], 6, v["ar0"])

    solve(1, remove(1, known, root_answer))
    for j, rows in enumerate(picked(1)):
        v["k1"][:, j] = rows.reshape(16, 8, 128)
    scatter_z(NZ, v["k1"], 8, v["kr1"])()
    v["kx1"][...] = total(v["kr1"])
    to_one(v["kx1"].at[1 - pair], v["kt1"], x_mate)()
    v["ks1"][...] = v["kx1"][pair] + v["kt1"][...]
    done = gather_z(NZ, v["ks1"], 8, v["z1"])
    done_a1 = to_one(v["s1"].at[rows_of(1 - pair, 192)], v["ax1"], x_mate)
    done()
    known = jnp.concatenate([v["z1"][...].reshape(B, 128), known], 0)

    def first_answer():
        done_a1()
        v["am1"][...] = v["s1"][rows_of(pair, 192), :] + v["ax1"][...]
        for p in range(16):
            v["ap1"][p] = v["am1"][12 * p : 12 * p + 12, :]
        answers[1] = scatter_z(NZ, v["ap1"], 12, v["ar1"])

    solve(2, remove(2, known, first_answer))
    for j, rows in enumerate(picked(2)):
        v["k2"][j * B : (j + 1) * B, :] = rows
    scatter_z(NZ, v["k2"], 16, v["kr2"])()
    v["ks2"][...] = total(v["kr2"])
    gather_z(8, v["ks2"], 16, v["z2"])()
    known = jnp.concatenate([v["z2"][...], known], 0)

    def second_answer():
        answers[2] = scatter_z(NZ, v["s2"], 24, v["ar2"])

    solve(3, remove(3, known, second_answer))
    for j, rows in enumerate(picked(3)):
        v["k3"][j * B : (j + 1) * B, :] = rows
    scatter_z(8, v["k3"], 32, v["kr3"])()
    v["ks3"][...] = total(v["kr3"])
    gather_z(4, v["ks3"], 32, v["z3"])()
    known = jnp.concatenate([v["z3"][...], known], 0)

    def third_answer():
        answers[3] = scatter_z(8, v["s3"], 48, v["ar3"])

    solve(4, remove(4, known, third_answer))
    answers[4] = scatter_z(4, v["s4"], 96, v["ar4"])
    for level in range(LEVELS):
        answers[level]()
        outs[level][0, 0] = total(v[f"ar{level}"])
    for like, k in sent:
        await_bytes(like, k, send_sems)


def per_device(added_rows, r0, r1, r2, r3, r4, g0, g1, g2, g3, g4, p1, p2, p3, p4):
    vmem = pl.BlockSpec(memory_space=pltpu.VMEM)
    return pl.pallas_call(
        kernel,
        out_shape=tuple(jax.ShapeDtypeStruct((1, 1, w, 128), jnp.float32) for w in OWN),
        in_specs=[pl.BlockSpec(memory_space=pltpu.SMEM)] + [pl.BlockSpec(memory_space=pl.ANY)] * 14,
        out_specs=(vmem,) * 5,
        scratch_shapes=[pltpu.VMEM(shape, jnp.float32) for shape in SCRATCH.values()]
        + [pltpu.VMEM(shape, jnp.bfloat16) for shape in MATRICES.values()]
        + [pltpu.VMEM((w, 128), jnp.float32) for w in OWN]
        + [pltpu.SemaphoreType.DMA((SEMS,)), pltpu.SemaphoreType.DMA((SEMS,)), pltpu.SemaphoreType.DMA((14,))],
        compiler_params=pltpu.CompilerParams(
            collective_id=0, has_side_effects=True, vmem_limit_bytes=57 * 2**20
        ),
        cost_estimate=pl.CostEstimate(flops=1_200_000_000, bytes_accessed=3_000_000, transcendentals=0),
        name="solve",
    )(added_rows.transpose(1, 2, 0), r0.transpose(0, 2, 1, 3), r1.transpose(0, 2, 1, 3), r2, r3, r4, g0, g1, g2, g3, g4, p1.T, p2.T, p3, p4)


def solution(mesh):
    rights, inverses, panels = P("front", "leaf", None, None), P("leaf", "front"), P("front", "leaf")
    return jax.shard_map(
        per_device,
        mesh=mesh,
        in_specs=(P(),) + (rights,) * 5 + (inverses,) * 5 + (panels,) * 4,
        out_specs=(rights,) * 5,
        check_vma=False,
    )
```

```python
import jax
import jax.numpy as jnp
from jax import lax
from jax.experimental import pallas as pl
from jax.experimental.pallas import tpu as pltpu
from jax.sharding import PartitionSpec as P

MESH = pl.DeviceIdType.MESH
B = 128
LEVELS = 5
NZ = 16
NX = 4
NY = 4
SLAB = 384
ROWS = (192, 192, 192, 384, 768)
OWN = (6, 12, 24, 48, 96)

SCRATCH = {
    "b0": (4, 16, 6, 128), "b1": (2, 16, 12, 128), "b2": (SLAB, 128), "b3": (SLAB, 128), "c4": (SLAB, 128),
    "c3": (SLAB, 128), "c2": (SLAB, 128), "c1": (SLAB, 128), "c0": (SLAB, 128),
    "t0": (4, 48, 384), "t1": (2, 96, 384), "tp": (2, 96, 128),
    "u4": (512, 128), "u3": (384, 128), "u2": (256, 128), "u2x": (128, 128), "u1": (128, 128),
    "ur4": (4, 32, 128), "us4": (32, 128), "ug4": (256, 128),
    "ur3": (8, 16, 128), "us3": (16, 128), "ug3": (256, 128),
    "ur2": (16, 8, 128), "us2": (8, 128), "ug2": (2, 16, 8, 128),
    "ur1": (16, 8, 128), "us1": (8, 128), "ug1": (2, 16, 8, 128),
    "s0": (SLAB, 128), "s1": (SLAB, 128), "s2": (SLAB, 128), "s3": (SLAB, 128), "s4": (SLAB, 128),
    "k0": (128, 128), "kr0": (16, 8, 128), "ks0": (8, 128), "z0": (128, 128),
    "k1": (128, 128), "kr1": (16, 8, 128), "ks1": (8, 128), "z1": (128, 128),
    "k2": (256, 128), "kr2": (16, 16, 128), "ks2": (16, 128), "z2": (128, 128),
    "k3": (256, 128), "kr3": (8, 32, 128), "ks3": (32, 128), "z3": (128, 128),
    "ar4": (4, 96, 128), "ar3": (8, 48, 128), "ar2": (16, 24, 128),
    "am1": (192, 128), "ap1": (16, 12, 128), "ar1": (16, 12, 128),
    "am0": (96, 128), "ap0": (16, 6, 128), "ar0": (16, 6, 128),
}
for _way in "fb":
    for _l in range(LEVELS):
        _h = ROWS[_l] // 2
        SCRATCH[f"{_way}p{_l}"] = (2 * _h, 128)
        SCRATCH[f"{_way}c{_l}"] = (_h, 128)
        SCRATCH[f"{_way}h{_l}"] = (_h, 128)
        if _l >= 3:
            SCRATCH[f"{_way}r{_l}"] = (4, _h // 4, 128)
            SCRATCH[f"{_way}q{_l}"] = (_h // 4, 128)
            SCRATCH[f"{_way}g{_l}"] = (_h, 128)
        else:
            SCRATCH[f"{_way}r{_l}"] = (4, _h, 128)
            SCRATCH[f"{_way}g{_l}"] = (_h, 128)
        SCRATCH[f"{_way}y{_l}"] = (2 * _h, 128)
NAMES = tuple(SCRATCH)
SEMS = 128
MATRICES = {
    "g0x": (48, 384), "g1x": (96, 384), "g2": (192, 384), "g3": (384, 384), "g4": (768, 384),
    "q1x": (96, 128), "q2": (192, 256), "p3": (384, 384), "p4": (512, 768),
    "g0": (192, 384), "g1": (192, 384), "q1": (192, 128),
    "h0": (384, 192), "h1": (384, 192), "h2": (384, 192), "h3": (384, 384), "h4": (384, 768),
    "p1": (128, 192), "p2": (256, 192), "q3": (384, 384), "q4": (768, 512),
}
LOADED = tuple(MATRICES)[:9]


def split(values):
    high = values.astype(jnp.bfloat16)
    low = (values - high.astype(jnp.float32)).astype(jnp.bfloat16)
    return jnp.concatenate([high, low], axis=1)


def times(matrix, values):
    both = jnp.dot(matrix, split(values), preferred_element_type=jnp.float32)
    return both[:, :128] + both[:, 128:]


def rows_of(index, count):
    return pl.ds(pl.multiple_of(index * count, 8), count)


def total(ref):
    parts = [ref[j] for j in range(ref.shape[0])]
    while len(parts) > 1:
        parts = [parts[j] + parts[j + 1] for j in range(0, len(parts), 2)]
    return parts[0]


def kernel(added, *refs):
    stored_rights, refs = refs[:5], refs[5:]
    stored, refs = refs[:9], refs[9:]
    outs, refs = refs[:5], refs[5:]
    v = dict(zip(NAMES, refs[: len(NAMES)]))
    refs = refs[len(NAMES) :]
    m = dict(zip(MATRICES, refs[: len(MATRICES)]))
    rights, refs = refs[len(MATRICES) : len(MATRICES) + 5], refs[len(MATRICES) + 5 :]
    send_sems, recv_sems, load_sems = refs

    leaf = lax.axis_index("leaf")
    front = lax.axis_index("front")
    x, z = leaf // NZ, leaf % NZ
    y, core = front // 2, front % 2
    pair = x % 2

    counter = [0]
    sent = []

    def at_z(n, i):
        d = n // 2 + (i + 1) // 2 * (1 - 2 * (i % 2))
        there = (z % n + d) % n
        return there, (x * NZ + z - z % n + there, front)

    def at_x(d):
        other = (x + d) % NX
        return other, (other * NZ + z, front)

    x_mate = ((x + 1 - 2 * pair) * NZ + z, front)
    core_mate = (leaf, front + 1 - 2 * core)

    def at_y(d):
        other = (y + d) % NY
        return other, (leaf, other * 2 + core)

    def begin():
        counter[0] += 1
        return counter[0] - 1

    def send(src, dst, k, device):
        pltpu.make_async_remote_copy(
            src_ref=src, dst_ref=dst, send_sem=send_sems.at[k], recv_sem=recv_sems.at[k],
            device_id=device, device_id_type=MESH,
        ).start()

    def await_bytes(like, k, sems):
        pltpu.make_async_copy(like, like, sems.at[k]).wait()

    def scatter_z(n, src, rows, dst):
        k = begin()
        whole_pieces = len(src.shape) > 2

        def piece(i):
            return src.at[i] if whole_pieces else src.at[rows_of(i, rows)]

        def step(i, _):
            there, device = at_z(n, i)
            send(piece(there), dst.at[z % n], k, device)
            return 0

        lax.fori_loop(0, n - 1, step, 0)
        here = z % n
        dst[here] = src[here] if whole_pieces else src[rows_of(here, rows), :]
        like = dst.at[pl.ds(0, n - 1)]
        sent.append((like, k))
        return lambda: await_bytes(like, k, recv_sems)

    def gather_z(n, src, rows, dst):
        k = begin()
        whole_pieces = len(dst.shape) > 2
        here = z % n
        spot = dst.at[here] if whole_pieces else dst.at[rows_of(here, rows)]

        def step(i, _):
            _, device = at_z(n, i)
            send(src, spot, k, device)
            return 0

        lax.fori_loop(0, n - 1, step, 0)
        if whole_pieces:
            dst[here] = src[...]
        else:
            dst[rows_of(here, rows), :] = src[...]
        like = dst.at[pl.ds(0, (n - 1) if whole_pieces else (n - 1) * rows)]
        sent.append((like, k))
        return lambda: await_bytes(like, k, recv_sems)

    def gather_xz(src, dst, slot, other_x):
        k, k_other = begin(), begin()

        def step(i, _):
            there, device = at_z(NZ, i)
            send(src, dst.at[slot, z], k_other, (other_x * NZ + there, front))
            send(src, dst.at[slot, z], k, device)
            return 0

        lax.fori_loop(0, NZ - 1, step, 0)
        send(src, dst.at[slot, z], k_other, (other_x * NZ + z, front))
        dst[slot, z] = src[...]
        sent.append((dst.at[0, pl.ds(0, NZ - 1)], k))
        sent.append((dst.at[0], k_other))

        def done():
            await_bytes(dst.at[0, pl.ds(0, NZ - 1)], k, recv_sems)
            await_bytes(dst.at[0], k_other, recv_sems)

        return done

    def to_one(src, dst, device):
        k = begin()
        send(src, dst, k, device)
        sent.append((dst, k))
        return lambda: await_bytes(dst, k, recv_sems)

    def to_x(pieces, dst):
        k = begin()
        for d in (2, 1, 3):
            other, device = at_x(d)
            send(pieces(other), dst.at[x], k, device)
        like = dst.at[pl.ds(0, 3)]
        sent.append((like, k))
        return lambda: await_bytes(like, k, recv_sems)

    def to_y(pieces, spot, like):
        k = begin()
        for d in (2, 1, 3):
            other, device = at_y(d)
            send(pieces(other), spot, k, device)
        sent.append((like, k))
        return lambda: await_bytes(like, k, recv_sems)

    def front_sum(way, level, meanwhile=None):
        term, half, whole = v[f"{way}p{level}"], v[f"{way}h{level}"], v[f"{way}y{level}"]
        received, summed = v[f"{way}r{level}"], v[f"{way}g{level}"]
        h = ROWS[level] // 2
        from_core = v[f"{way}c{level}"]
        done = to_one(term.at[rows_of(1 - core, h)], from_core, core_mate)
        done()
        half[...] = term[rows_of(core, h), :] + from_core[...]
        if level >= 3:
            q = h // 4
            piece = v[f"{way}q{level}"]
            done = to_y(lambda other: half.at[rows_of(other, q)], received.at[y], received.at[pl.ds(0, 3)])
            received[y] = half[rows_of(y, q), :]
            if meanwhile is not None:
                meanwhile()
            done()
            piece[...] = total(received)
            done = to_y(lambda other: piece, summed.at[rows_of(y, q)], summed.at[pl.ds(0, 3 * q)])
            summed[rows_of(y, q), :] = piece[...]
            done()
        else:
            done = to_y(lambda other: half, received.at[y], received.at[pl.ds(0, 3)])
            received[y] = half[...]
            if meanwhile is not None:
                meanwhile()
            done()
            summed[...] = total(received)
        done = to_one(summed, whole.at[rows_of(core, h)], core_mate)
        whole[rows_of(core, h), :] = summed[...]
        done()
        return whole

    def choice(level, child):
        block = added[front, 0, 2 ** (level + 1) - 2 + child]
        return [jnp.where(block == j, 1.0, 0.0).astype(jnp.float32) for j in range(3)]

    def choices(level):
        node = leaf // (64 >> level)
        return choice(level, 2 * node), choice(level, 2 * node + 1)

    def place(level, b, low, high):
        to_low, to_high = choices(level)
        target = v[f"c{level}"]
        for j in range(3):
            spot = slice(j * B, (j + 1) * B)
            target[spot, :] = b[spot, :] - low * to_low[j] - high * to_high[j]

    def pick(s, weights):
        return s[0:B, :] * weights[0] + s[B : 2 * B, :] * weights[1] + s[2 * B :, :] * weights[2]

    loads = {}

    def load(name, src, dst, k):
        copy = pltpu.make_async_copy(src, dst, load_sems.at[k])
        copy.start()
        loads[name] = copy.wait

    load("r4", stored_rights[4].at[0, 0], rights[4], 4)
    load("g4", stored[4], m["g4"], 9)
    for level in (3, 2):
        load(f"r{level}", stored_rights[level].at[0, 0], rights[level], level)
    for level in (1, 0):
        for i in range(OWN[level]):
            pltpu.make_async_copy(
                stored_rights[level].at[0, i], rights[level].at[pl.ds(i, 1)], load_sems.at[level]
            ).start()
    for k, name in enumerate(LOADED):
        if name != "g4":
            load(name, stored[k], m[name], 5 + k)

    barrier = pltpu.get_barrier_semaphore()

    def greet(device):
        pl.semaphore_signal(barrier, inc=1, device_id=device, device_id_type=MESH)

    greet((x * NZ + (z + 4) % NZ, front))
    greet((x * NZ + (z + 12) % NZ, front))
    for i in range(3):
        greet(at_z(4, i)[1])
    for d in (1, 2, 3):
        greet(at_x(d)[1])
        greet(at_y(d)[1])
    greet(core_mate)
    pl.semaphore_wait(barrier, 12)

    loads["r4"]()
    done_b4 = gather_z(4, rights[4], 96, v["c4"])
    await_bytes(rights[1], 1, load_sems)
    await_bytes(rights[0], 0, load_sems)
    for name in ("r3", "r2") + LOADED:
        loads[name]()
    v["t0"][x] = m["g0x"][...].astype(jnp.float32)
    v["t1"][pair] = m["g1x"][...].astype(jnp.float32)
    v["tp"][pair] = m["q1x"][...].astype(jnp.float32)
    done_tiles = [
        to_x(lambda other: v["t0"].at[x], v["t0"]),
        to_one(v["t1"].at[pair], v["t1"].at[pair], x_mate),
        to_one(v["tp"].at[pair], v["tp"].at[pair], x_mate),
    ]
    done_b = {}

    def turn(*names):
        for source, target in names:
            m[target][...] = m[source][...].T

    def more_b3():
        done_b[3] = gather_z(8, rights[3], 48, v["b3"])

    def more_b2():
        done_b[2] = gather_z(NZ, rights[2], 24, v["b2"])

    def more_b1():
        done_b[1] = gather_z(NZ, rights[1], 12, v["b1"].at[pair])

    def more_b0():
        done_b[0] = gather_z(NZ, rights[0], 6, v["b0"].at[x])

    turn(("g4", "h4"))
    done_b4()
    v["fp4"][...] = times(m["g4"][...], v["c4"][...])
    y4 = front_sum("f", 4, more_b3)
    v["u4"][...] = times(m["p4"][...], y4[...])
    done = scatter_z(4, v["u4"], 32, v["ur4"])
    turn(("p4", "q4"))
    done()
    v["us4"][...] = total(v["ur4"])
    done = gather_z(8, v["us4"], 32, v["ug4"])
    turn(("g3", "h3"), ("q2", "p2"))
    done_b[3]()
    done()

    place(3, v["b3"], v["ug4"][0:B, :], v["ug4"][B:, :])
    v["fp3"][...] = times(m["g3"][...], v["c3"][...])
    y3 = front_sum("f", 3, more_b2)
    v["u3"][...] = times(m["p3"][...], y3[...]) + v["u4"][B:, :]
    done = scatter_z(8, v["u3"], 16, v["ur3"])
    turn(("p3", "q3"))
    done()
    v["us3"][...] = total(v["ur3"])
    done = gather_z(NZ, v["us3"], 16, v["ug3"])
    for wait in done_tiles:
        wait()
    m["g0"][...] = v["t0"][...].reshape(192, 384).astype(jnp.bfloat16)
    m["g1"][...] = v["t1"][...].reshape(192, 384).astype(jnp.bfloat16)
    m["q1"][...] = v["tp"][...].reshape(192, 128).astype(jnp.bfloat16)
    turn(("g2", "h2"), ("g1", "h1"), ("g0", "h0"), ("q1", "p1"))
    done_b[2]()
    done()

    place(2, v["b2"], v["ug3"][0:B, :], v["ug3"][B:, :])
    v["fp2"][...] = times(m["g2"][...], v["c2"][...])
    y2 = front_sum("f", 2, more_b1)
    v["u2"][...] = times(m["p2"][...], y2[...]) + v["u3"][B:, :]
    scatter_z(NZ, v["u2"], 8, v["ur2"])()
    v["us2"][...] = total(v["ur2"])
    done = gather_xz(v["us2"], v["ug2"], pair, x + 1 - 2 * pair)
    done_u2x = to_one(v["u2"].at[pl.ds(B, B)], v["u2x"], x_mate)
    done_b[1]()
    to_one(v["b1"].at[pair], v["b1"].at[pair], x_mate)()
    for p in range(32):
        v["c1"][12 * p : 12 * p + 12, :] = v["b1"][p // 16, p % 16]
    done()

    low, high = (v["ug2"][j].reshape(B, 128) for j in range(2))
    place(1, v["c1"], low, high)
    v["fp1"][...] = times(m["g1"][...], v["c1"][...])
    y1 = front_sum("f", 1, more_b0)
    done_u2x()
    v["u1"][...] = times(m["p1"][...], y1[...]) + (v["u2"][B:, :] + v["u2x"][...])
    scatter_z(NZ, v["u1"], 8, v["ur1"])()
    v["us1"][...] = total(v["ur1"])
    done = gather_xz(v["us1"], v["ug1"], x // 2, (x + 2) % NX)
    done_b[0]()
    to_x(lambda other: v["b0"].at[x], v["b0"])()
    for p in range(64):
        v["c0"][6 * p : 6 * p + 6, :] = v["b0"][p // 16, p % 16]
    done()

    low, high = (v["ug1"][j].reshape(B, 128) for j in range(2))
    place(0, v["c0"], low, high)
    v["fp0"][...] = times(m["g0"][...], v["c0"][...])
    y0 = front_sum("f", 0)

    def solve(level, right_side):
        v[f"s{level}"][...] = times(m[f"h{level}"][...], right_side)

    def picked(level):
        to_low, to_high = choices(level)
        s = v[f"s{level}"]
        return pick(s, to_low), pick(s, to_high)

    def remove(level, known, meanwhile=None):
        v[f"bp{level}"][...] = times(m[f"q{level}"][...], known)
        through = front_sum("b", level, meanwhile)
        return v[f"fy{level}"][...] - through[...]

    answers = {}
    solve(0, y0[...])
    v["k0"][...] = pick(v["s0"], choice(0, x // 2))
    scatter_z(NZ, v["k0"], 8, v["kr0"])()
    v["ks0"][...] = total(v["kr0"])
    gather_z(NZ, v["ks0"], 8, v["z0"])()
    known = v["z0"][...]

    def root_answer():
        v["am0"][...] = v["s0"][rows_of(x, 96), :]
        for p in range(16):
            v["ap0"][p] = v["am0"][6 * p : 6 * p + 6, :]
        answers[0] = scatter_z(NZ, v["ap0"], 6, v["ar0"])

    solve(1, remove(1, known, root_answer))
    v["k1"][...] = pick(v["s1"], choice(1, x))
    scatter_z(NZ, v["k1"], 8, v["kr1"])()
    v["ks1"][...] = total(v["kr1"])
    gather_z(NZ, v["ks1"], 8, v["z1"])()
    known = jnp.concatenate([v["z1"][...], known], 0)

    def first_answer():
        v["am1"][...] = v["s1"][rows_of(pair, 192), :]
        for p in range(16):
            v["ap1"][p] = v["am1"][12 * p : 12 * p + 12, :]
        answers[1] = scatter_z(NZ, v["ap1"], 12, v["ar1"])

    solve(2, remove(2, known, first_answer))
    for j, rows in enumerate(picked(2)):
        v["k2"][j * B : (j + 1) * B, :] = rows
    scatter_z(NZ, v["k2"], 16, v["kr2"])()
    v["ks2"][...] = total(v["kr2"])
    gather_z(8, v["ks2"], 16, v["z2"])()
    known = jnp.concatenate([v["z2"][...], known], 0)

    def second_answer():
        answers[2] = scatter_z(NZ, v["s2"], 24, v["ar2"])

    solve(3, remove(3, known, second_answer))
    for j, rows in enumerate(picked(3)):
        v["k3"][j * B : (j + 1) * B, :] = rows
    scatter_z(8, v["k3"], 32, v["kr3"])()
    v["ks3"][...] = total(v["kr3"])
    gather_z(4, v["ks3"], 32, v["z3"])()
    known = jnp.concatenate([v["z3"][...], known], 0)

    def third_answer():
        answers[3] = scatter_z(8, v["s3"], 48, v["ar3"])

    solve(4, remove(4, known, third_answer))
    answers[4] = scatter_z(4, v["s4"], 96, v["ar4"])
    for level in range(LEVELS):
        answers[level]()
        outs[level][0, 0] = total(v[f"ar{level}"])
    for like, k in sent:
        await_bytes(like, k, send_sems)


def per_device(added_rows, r0, r1, r2, r3, r4, g0, g1, g2, g3, g4, p1, p2, p3, p4):
    vmem = pl.BlockSpec(memory_space=pltpu.VMEM)
    return pl.pallas_call(
        kernel,
        out_shape=tuple(jax.ShapeDtypeStruct((1, 1, w, 128), jnp.float32) for w in OWN),
        in_specs=[pl.BlockSpec(memory_space=pltpu.SMEM)] + [pl.BlockSpec(memory_space=pl.ANY)] * 14,
        out_specs=(vmem,) * 5,
        scratch_shapes=[pltpu.VMEM(shape, jnp.float32) for shape in SCRATCH.values()]
        + [pltpu.VMEM(shape, jnp.bfloat16) for shape in MATRICES.values()]
        + [pltpu.VMEM((w, 128), jnp.float32) for w in OWN]
        + [pltpu.SemaphoreType.DMA((SEMS,)), pltpu.SemaphoreType.DMA((SEMS,)), pltpu.SemaphoreType.DMA((14,))],
        compiler_params=pltpu.CompilerParams(
            collective_id=0, has_side_effects=True, vmem_limit_bytes=57 * 2**20
        ),
        cost_estimate=pl.CostEstimate(flops=1_200_000_000, bytes_accessed=3_000_000, transcendentals=0),
        name="solve",
    )(added_rows.transpose(1, 2, 0), r0.transpose(0, 2, 1, 3), r1.transpose(0, 2, 1, 3), r2, r3, r4, g0, g1, g2, g3, g4, p1.T, p2.T, p3, p4)


def solution(mesh):
    rights, inverses, panels = P("front", "leaf", None, None), P("leaf", "front"), P("front", "leaf")
    return jax.shard_map(
        per_device,
        mesh=mesh,
        in_specs=(P(),) + (rights,) * 5 + (inverses,) * 5 + (panels,) * 4,
        out_specs=(rights,) * 5,
        check_vma=False,
    )
```

```python
import jax
import jax.numpy as jnp
from jax import lax
from jax.experimental import pallas as pl
from jax.experimental.pallas import tpu as pltpu
from jax.sharding import PartitionSpec as P

MESH = pl.DeviceIdType.MESH
B = 128
LEVELS = 5
NZ = 16
NX = 4
NY = 4
SLAB = 384
ROWS = (192, 192, 192, 384, 768)
OWN = (6, 12, 24, 48, 96)

SCRATCH = {
    "b0": (4, 16, 6, 128), "b1": (2, 16, 12, 128), "b2": (SLAB, 128), "b3": (SLAB, 128), "c4": (SLAB, 128),
    "c3": (SLAB, 128), "c2": (SLAB, 128), "c1": (SLAB, 128), "c0": (SLAB, 128),
    "t0": (4, 48, 384), "t1": (2, 96, 384), "tp": (2, 96, 128),
    "u4": (512, 128), "u3": (384, 128), "u2": (256, 128), "u2x": (128, 128), "u1": (128, 128),
    "ur4": (4, 32, 128), "us4": (32, 128), "ug4": (256, 128),
    "ur3": (8, 16, 128), "us3": (16, 128), "ug3": (256, 128),
    "ur2": (16, 8, 128), "us2": (8, 128), "ug2": (2, 16, 8, 128),
    "ur1": (16, 8, 128), "us1": (8, 128), "ug1": (2, 16, 8, 128),
    "s0": (SLAB, 128), "s1": (SLAB, 128), "s2": (SLAB, 128), "s3": (SLAB, 128), "s4": (SLAB, 128),
    "k0": (128, 128), "kr0": (16, 8, 128), "ks0": (8, 128), "z0": (128, 128),
    "k1": (128, 128), "kr1": (16, 8, 128), "ks1": (8, 128), "z1": (128, 128),
    "k2": (256, 128), "kr2": (16, 16, 128), "ks2": (16, 128), "z2": (128, 128),
    "k3": (256, 128), "kr3": (8, 32, 128), "ks3": (32, 128), "z3": (128, 128),
    "ar4": (4, 96, 128), "ar3": (8, 48, 128), "ar2": (16, 24, 128),
    "am1": (192, 128), "ap1": (16, 12, 128), "ar1": (16, 12, 128),
    "am0": (96, 128), "ap0": (16, 6, 128), "ar0": (16, 6, 128),
}
for _way in "fb":
    for _l in range(LEVELS):
        _h = ROWS[_l] // 2
        SCRATCH[f"{_way}p{_l}"] = (2 * _h, 128)
        SCRATCH[f"{_way}c{_l}"] = (_h, 128)
        SCRATCH[f"{_way}h{_l}"] = (_h, 128)
        if _l >= 3:
            SCRATCH[f"{_way}r{_l}"] = (4, _h // 4, 128)
            SCRATCH[f"{_way}q{_l}"] = (_h // 4, 128)
            SCRATCH[f"{_way}g{_l}"] = (_h, 128)
        else:
            SCRATCH[f"{_way}r{_l}"] = (4, _h, 128)
            SCRATCH[f"{_way}g{_l}"] = (_h, 128)
        SCRATCH[f"{_way}y{_l}"] = (2 * _h, 128)
NAMES = tuple(SCRATCH)
SEMS = 128
MATRICES = {
    "g0x": (48, 384), "g1x": (96, 384), "g2": (192, 384), "g3": (384, 384), "g4": (768, 384),
    "q1x": (96, 128), "q2": (192, 256), "p3": (384, 384), "p4": (512, 768),
    "g0": (192, 384), "g1": (192, 384), "q1": (192, 128),
    "h0": (384, 192), "h1": (384, 192), "h2": (384, 192), "h3": (384, 384), "h4": (384, 768),
    "p1": (128, 192), "p2": (256, 192), "q3": (384, 384), "q4": (768, 512),
}
LOADED = tuple(MATRICES)[:9]


def split(values):
    high = values.astype(jnp.bfloat16)
    low = (values - high.astype(jnp.float32)).astype(jnp.bfloat16)
    return jnp.concatenate([high, low], axis=1)


def times(matrix, values):
    both = jnp.dot(matrix, split(values), preferred_element_type=jnp.float32)
    return both[:, :128] + both[:, 128:]


def rows_of(index, count):
    return pl.ds(pl.multiple_of(index * count, 8), count)


def total(ref):
    parts = [ref[j] for j in range(ref.shape[0])]
    while len(parts) > 1:
        parts = [parts[j] + parts[j + 1] for j in range(0, len(parts), 2)]
    return parts[0]


def kernel(added, *refs):
    stored_rights, refs = refs[:5], refs[5:]
    stored, refs = refs[:9], refs[9:]
    outs, refs = refs[:5], refs[5:]
    v = dict(zip(NAMES, refs[: len(NAMES)]))
    refs = refs[len(NAMES) :]
    m = dict(zip(MATRICES, refs[: len(MATRICES)]))
    rights, refs = refs[len(MATRICES) : len(MATRICES) + 5], refs[len(MATRICES) + 5 :]
    send_sems, recv_sems, load_sems = refs

    leaf = lax.axis_index("leaf")
    front = lax.axis_index("front")
    x, z = lax.div(leaf, NZ), lax.rem(leaf, NZ)
    y, core = lax.div(front, 2), lax.rem(front, 2)
    pair = lax.rem(x, 2)

    counter = [0]
    sent = []

    def each_z(n, act):
        here = lax.rem(z, n)
        start = leaf - here

        def partner(d):
            there = lax.rem(here + d, n)
            act(there, start + there)

        def step(k, _):
            partner(n // 2 - k)
            partner(n // 2 + k)
            return 0

        partner(n // 2)
        lax.fori_loop(1, n // 2, step, 0)

    def at_x(d):
        other = lax.rem(x + d, NX)
        return other, (other * NZ + z, front)

    x_mate = ((x + 1 - 2 * pair) * NZ + z, front)
    core_mate = (leaf, front + 1 - 2 * core)

    def at_y(d):
        other = lax.rem(y + d, NY)
        return other, (leaf, other * 2 + core)

    def begin():
        counter[0] += 1
        return counter[0] - 1

    def send(src, dst, k, device):
        pltpu.make_async_remote_copy(
            src_ref=src, dst_ref=dst, send_sem=send_sems.at[k], recv_sem=recv_sems.at[k],
            device_id=device, device_id_type=MESH,
        ).start()

    def await_bytes(like, k, sems):
        pltpu.make_async_copy(like, like, sems.at[k]).wait()

    def scatter_z(n, src, rows, dst):
        k = begin()
        whole_pieces = len(src.shape) > 2

        def piece(i):
            return src.at[i] if whole_pieces else src.at[rows_of(i, rows)]

        here = lax.rem(z, n)
        each_z(n, lambda there, device: send(piece(there), dst.at[here], k, (device, front)))
        dst[here] = src[here] if whole_pieces else src[rows_of(here, rows), :]
        like = dst.at[pl.ds(0, n - 1)]
        sent.append((like, k))
        return lambda: await_bytes(like, k, recv_sems)

    def gather_z(n, src, rows, dst):
        k = begin()
        whole_pieces = len(dst.shape) > 2
        here = lax.rem(z, n)
        spot = dst.at[here] if whole_pieces else dst.at[rows_of(here, rows)]

        each_z(n, lambda there, device: send(src, spot, k, (device, front)))
        if whole_pieces:
            dst[here] = src[...]
        else:
            dst[rows_of(here, rows), :] = src[...]
        like = dst.at[pl.ds(0, (n - 1) if whole_pieces else (n - 1) * rows)]
        sent.append((like, k))
        return lambda: await_bytes(like, k, recv_sems)

    def gather_xz(src, dst, slot, other_x):
        k, k_other = begin(), begin()

        def both(there, device):
            send(src, dst.at[slot, z], k_other, (other_x * NZ + there, front))
            send(src, dst.at[slot, z], k, (device, front))

        each_z(NZ, both)
        send(src, dst.at[slot, z], k_other, (other_x * NZ + z, front))
        dst[slot, z] = src[...]
        sent.append((dst.at[0, pl.ds(0, NZ - 1)], k))
        sent.append((dst.at[0], k_other))

        def done():
            await_bytes(dst.at[0, pl.ds(0, NZ - 1)], k, recv_sems)
            await_bytes(dst.at[0], k_other, recv_sems)

        return done

    def to_one(src, dst, device):
        k = begin()
        send(src, dst, k, device)
        sent.append((dst, k))
        return lambda: await_bytes(dst, k, recv_sems)

    def to_x(pieces, dst):
        k = begin()
        for d in (2, 1, 3):
            other, device = at_x(d)
            send(pieces(other), dst.at[x], k, device)
        like = dst.at[pl.ds(0, 3)]
        sent.append((like, k))
        return lambda: await_bytes(like, k, recv_sems)

    def to_y(pieces, spot, like):
        k = begin()
        for d in (2, 1, 3):
            other, device = at_y(d)
            send(pieces(other), spot, k, device)
        sent.append((like, k))
        return lambda: await_bytes(like, k, recv_sems)

    def front_sum(way, level, meanwhile=None):
        term, half, whole = v[f"{way}p{level}"], v[f"{way}h{level}"], v[f"{way}y{level}"]
        received, summed = v[f"{way}r{level}"], v[f"{way}g{level}"]
        h = ROWS[level] // 2
        from_core = v[f"{way}c{level}"]
        done = to_one(term.at[rows_of(1 - core, h)], from_core, core_mate)
        done()
        half[...] = term[rows_of(core, h), :] + from_core[...]
        if level >= 3:
            q = h // 4
            piece = v[f"{way}q{level}"]
            done = to_y(lambda other: half.at[rows_of(other, q)], received.at[y], received.at[pl.ds(0, 3)])
            received[y] = half[rows_of(y, q), :]
            if meanwhile is not None:
                meanwhile()
            done()
            piece[...] = total(received)
            done = to_y(lambda other: piece, summed.at[rows_of(y, q)], summed.at[pl.ds(0, 3 * q)])
            summed[rows_of(y, q), :] = piece[...]
            done()
        else:
            done = to_y(lambda other: half, received.at[y], received.at[pl.ds(0, 3)])
            received[y] = half[...]
            if meanwhile is not None:
                meanwhile()
            done()
            summed[...] = total(received)
        done = to_one(summed, whole.at[rows_of(core, h)], core_mate)
        whole[rows_of(core, h), :] = summed[...]
        done()
        return whole

    def choice(level, child):
        block = added[front, 0, 2 ** (level + 1) - 2 + child]
        return [jnp.where(block == j, 1.0, 0.0).astype(jnp.float32) for j in range(3)]

    def choices(level):
        node = leaf // (64 >> level)
        return choice(level, 2 * node), choice(level, 2 * node + 1)

    def place(level, b, low, high):
        to_low, to_high = choices(level)
        target = v[f"c{level}"]
        for j in range(3):
            spot = slice(j * B, (j + 1) * B)
            target[spot, :] = b[spot, :] - low * to_low[j] - high * to_high[j]

    def pick(s, weights):
        return s[0:B, :] * weights[0] + s[B : 2 * B, :] * weights[1] + s[2 * B :, :] * weights[2]

    loads = {}

    def load(name, src, dst, k):
        copy = pltpu.make_async_copy(src, dst, load_sems.at[k])
        copy.start()
        loads[name] = copy.wait

    load("r4", stored_rights[4].at[0, 0], rights[4], 4)
    load("g4", stored[4], m["g4"], 9)
    for level in (3, 2):
        load(f"r{level}", stored_rights[level].at[0, 0], rights[level], level)
    for level in (1, 0):
        for i in range(OWN[level]):
            pltpu.make_async_copy(
                stored_rights[level].at[0, i], rights[level].at[pl.ds(i, 1)], load_sems.at[level]
            ).start()
    for k, name in enumerate(LOADED):
        if name != "g4":
            load(name, stored[k], m[name], 5 + k)

    barrier = pltpu.get_barrier_semaphore()

    def greet(device):
        pl.semaphore_signal(barrier, inc=1, device_id=device, device_id_type=MESH)

    greet((x * NZ + (z + 4) % NZ, front))
    greet((x * NZ + (z + 12) % NZ, front))
    each_z(4, lambda there, device: greet((device, front)))
    for d in (1, 2, 3):
        greet(at_x(d)[1])
        greet(at_y(d)[1])
    greet(core_mate)
    pl.semaphore_wait(barrier, 12)

    loads["r4"]()
    done_b4 = gather_z(4, rights[4], 96, v["c4"])
    await_bytes(rights[1], 1, load_sems)
    await_bytes(rights[0], 0, load_sems)
    for name in ("r3", "r2") + LOADED:
        loads[name]()
    v["t0"][x] = m["g0x"][...].astype(jnp.float32)
    v["t1"][pair] = m["g1x"][...].astype(jnp.float32)
    v["tp"][pair] = m["q1x"][...].astype(jnp.float32)
    done_tiles = [
        to_x(lambda other: v["t0"].at[x], v["t0"]),
        to_one(v["t1"].at[pair], v["t1"].at[pair], x_mate),
        to_one(v["tp"].at[pair], v["tp"].at[pair], x_mate),
    ]
    done_b = {}

    def turn(*names):
        for source, target in names:
            m[target][...] = m[source][...].T

    def more_b3():
        done_b[3] = gather_z(8, rights[3], 48, v["b3"])

    def more_b2():
        done_b[2] = gather_z(NZ, rights[2], 24, v["b2"])

    def more_b1():
        done_b[1] = gather_z(NZ, rights[1], 12, v["b1"].at[pair])

    def more_b0():
        done_b[0] = gather_z(NZ, rights[0], 6, v["b0"].at[x])

    turn(("g4", "h4"))
    done_b4()
    v["fp4"][...] = times(m["g4"][...], v["c4"][...])
    y4 = front_sum("f", 4, more_b3)
    v["u4"][...] = times(m["p4"][...], y4[...])
    done = scatter_z(4, v["u4"], 32, v["ur4"])
    turn(("p4", "q4"))
    done()
    v["us4"][...] = total(v["ur4"])
    done = gather_z(8, v["us4"], 32, v["ug4"])
    turn(("g3", "h3"), ("q2", "p2"))
    done_b[3]()
    done()

    place(3, v["b3"], v["ug4"][0:B, :], v["ug4"][B:, :])
    v["fp3"][...] = times(m["g3"][...], v["c3"][...])
    y3 = front_sum("f", 3, more_b2)
    v["u3"][...] = times(m["p3"][...], y3[...]) + v["u4"][B:, :]
    done = scatter_z(8, v["u3"], 16, v["ur3"])
    turn(("p3", "q3"))
    done()
    v["us3"][...] = total(v["ur3"])
    done = gather_z(NZ, v["us3"], 16, v["ug3"])
    for wait in done_tiles:
        wait()
    m["g0"][...] = v["t0"][...].reshape(192, 384).astype(jnp.bfloat16)
    m["g1"][...] = v["t1"][...].reshape(192, 384).astype(jnp.bfloat16)
    m["q1"][...] = v["tp"][...].reshape(192, 128).astype(jnp.bfloat16)
    turn(("g2", "h2"), ("g1", "h1"), ("g0", "h0"), ("q1", "p1"))
    done_b[2]()
    done()

    place(2, v["b2"], v["ug3"][0:B, :], v["ug3"][B:, :])
    v["fp2"][...] = times(m["g2"][...], v["c2"][...])
    y2 = front_sum("f", 2, more_b1)
    v["u2"][...] = times(m["p2"][...], y2[...]) + v["u3"][B:, :]
    scatter_z(NZ, v["u2"], 8, v["ur2"])()
    v["us2"][...] = total(v["ur2"])
    done = gather_xz(v["us2"], v["ug2"], pair, x + 1 - 2 * pair)
    done_u2x = to_one(v["u2"].at[pl.ds(B, B)], v["u2x"], x_mate)
    done_b[1]()
    to_one(v["b1"].at[pair], v["b1"].at[pair], x_mate)()
    for p in range(32):
        v["c1"][12 * p : 12 * p + 12, :] = v["b1"][p // 16, p % 16]
    done()

    low, high = (v["ug2"][j].reshape(B, 128) for j in range(2))
    place(1, v["c1"], low, high)
    v["fp1"][...] = times(m["g1"][...], v["c1"][...])
    y1 = front_sum("f", 1, more_b0)
    done_u2x()
    v["u1"][...] = times(m["p1"][...], y1[...]) + (v["u2"][B:, :] + v["u2x"][...])
    scatter_z(NZ, v["u1"], 8, v["ur1"])()
    v["us1"][...] = total(v["ur1"])
    done = gather_xz(v["us1"], v["ug1"], x // 2, (x + 2) % NX)
    done_b[0]()
    to_x(lambda other: v["b0"].at[x], v["b0"])()
    for p in range(64):
        v["c0"][6 * p : 6 * p + 6, :] = v["b0"][p // 16, p % 16]
    done()

    low, high = (v["ug1"][j].reshape(B, 128) for j in range(2))
    place(0, v["c0"], low, high)
    v["fp0"][...] = times(m["g0"][...], v["c0"][...])
    y0 = front_sum("f", 0)

    def solve(level, right_side):
        v[f"s{level}"][...] = times(m[f"h{level}"][...], right_side)

    def picked(level):
        to_low, to_high = choices(level)
        s = v[f"s{level}"]
        return pick(s, to_low), pick(s, to_high)

    def remove(level, known, meanwhile=None):
        v[f"bp{level}"][...] = times(m[f"q{level}"][...], known)
        through = front_sum("b", level, meanwhile)
        return v[f"fy{level}"][...] - through[...]

    answers = {}
    solve(0, y0[...])
    v["k0"][...] = pick(v["s0"], choice(0, x // 2))
    scatter_z(NZ, v["k0"], 8, v["kr0"])()
    v["ks0"][...] = total(v["kr0"])
    gather_z(NZ, v["ks0"], 8, v["z0"])()
    known = v["z0"][...]

    def root_answer():
        v["am0"][...] = v["s0"][rows_of(x, 96), :]
        for p in range(16):
            v["ap0"][p] = v["am0"][6 * p : 6 * p + 6, :]
        answers[0] = scatter_z(NZ, v["ap0"], 6, v["ar0"])

    solve(1, remove(1, known, root_answer))
    v["k1"][...] = pick(v["s1"], choice(1, x))
    scatter_z(NZ, v["k1"], 8, v["kr1"])()
    v["ks1"][...] = total(v["kr1"])
    gather_z(NZ, v["ks1"], 8, v["z1"])()
    known = jnp.concatenate([v["z1"][...], known], 0)

    def first_answer():
        v["am1"][...] = v["s1"][rows_of(pair, 192), :]
        for p in range(16):
            v["ap1"][p] = v["am1"][12 * p : 12 * p + 12, :]
        answers[1] = scatter_z(NZ, v["ap1"], 12, v["ar1"])

    solve(2, remove(2, known, first_answer))
    for j, rows in enumerate(picked(2)):
        v["k2"][j * B : (j + 1) * B, :] = rows
    scatter_z(NZ, v["k2"], 16, v["kr2"])()
    v["ks2"][...] = total(v["kr2"])
    gather_z(8, v["ks2"], 16, v["z2"])()
    known = jnp.concatenate([v["z2"][...], known], 0)

    def second_answer():
        answers[2] = scatter_z(NZ, v["s2"], 24, v["ar2"])

    solve(3, remove(3, known, second_answer))
    for j, rows in enumerate(picked(3)):
        v["k3"][j * B : (j + 1) * B, :] = rows
    scatter_z(8, v["k3"], 32, v["kr3"])()
    v["ks3"][...] = total(v["kr3"])
    gather_z(4, v["ks3"], 32, v["z3"])()
    known = jnp.concatenate([v["z3"][...], known], 0)

    def third_answer():
        answers[3] = scatter_z(8, v["s3"], 48, v["ar3"])

    solve(4, remove(4, known, third_answer))
    answers[4] = scatter_z(4, v["s4"], 96, v["ar4"])
    for level in range(LEVELS):
        answers[level]()
        outs[level][0, 0] = total(v[f"ar{level}"])
    for like, k in sent:
        await_bytes(like, k, send_sems)


def per_device(added_rows, r0, r1, r2, r3, r4, g0, g1, g2, g3, g4, p1, p2, p3, p4):
    vmem = pl.BlockSpec(memory_space=pltpu.VMEM)
    return pl.pallas_call(
        kernel,
        out_shape=tuple(jax.ShapeDtypeStruct((1, 1, w, 128), jnp.float32) for w in OWN),
        in_specs=[pl.BlockSpec(memory_space=pltpu.SMEM)] + [pl.BlockSpec(memory_space=pl.ANY)] * 14,
        out_specs=(vmem,) * 5,
        scratch_shapes=[pltpu.VMEM(shape, jnp.float32) for shape in SCRATCH.values()]
        + [pltpu.VMEM(shape, jnp.bfloat16) for shape in MATRICES.values()]
        + [pltpu.VMEM((w, 128), jnp.float32) for w in OWN]
        + [pltpu.SemaphoreType.DMA((SEMS,)), pltpu.SemaphoreType.DMA((SEMS,)), pltpu.SemaphoreType.DMA((14,))],
        compiler_params=pltpu.CompilerParams(
            collective_id=0, has_side_effects=True, vmem_limit_bytes=57 * 2**20
        ),
        cost_estimate=pl.CostEstimate(flops=1_200_000_000, bytes_accessed=3_000_000, transcendentals=0),
        name="solve",
    )(added_rows.transpose(1, 2, 0), r0.transpose(0, 2, 1, 3), r1.transpose(0, 2, 1, 3), r2, r3, r4, g0, g1, g2, g3, g4, p1.T, p2.T, p3, p4)


def solution(mesh):
    rights, inverses, panels = P("front", "leaf", None, None), P("leaf", "front"), P("front", "leaf")
    return jax.shard_map(
        per_device,
        mesh=mesh,
        in_specs=(P(),) + (rights,) * 5 + (inverses,) * 5 + (panels,) * 4,
        out_specs=(rights,) * 5,
        check_vma=False,
    )
```

```python
import jax
import jax.numpy as jnp
from jax import lax
from jax.experimental import pallas as pl
from jax.experimental.pallas import tpu as pltpu
from jax.sharding import PartitionSpec as P

MESH = pl.DeviceIdType.MESH
B = 128
LEVELS = 5
NZ = 16
NX = 4
NY = 4
SLAB = 384
ROWS = (192, 192, 192, 384, 768)
OWN = (6, 12, 24, 48, 96)

SCRATCH = {
    "b0": (4, 16, 6, 128), "b1": (2, 16, 12, 128), "b2": (SLAB, 128), "b3": (SLAB, 128), "c4": (SLAB, 128),
    "c3": (SLAB, 128), "c2": (SLAB, 128), "c1": (SLAB, 128), "c0": (SLAB, 128),
    "t0": (4, 48, 384), "t1": (2, 96, 384), "tp": (2, 96, 128),
    "u4": (512, 128), "u3": (384, 128), "u2": (256, 128), "u2x": (128, 128), "u1": (128, 128),
    "ur4": (4, 32, 128), "us4": (32, 128), "ug4": (256, 128),
    "ur3": (8, 16, 128), "us3": (16, 128), "ug3": (256, 128),
    "ur2": (16, 8, 128), "us2": (8, 128), "ug2": (2, 16, 8, 128),
    "ur1": (16, 8, 128), "us1": (8, 128), "ug1": (2, 16, 8, 128),
    "s0": (SLAB, 128), "s1": (SLAB, 128), "s2": (SLAB, 128), "s3": (SLAB, 128), "s4": (SLAB, 128),
    "k0": (128, 128), "kr0": (16, 8, 128), "ks0": (8, 128), "z0": (128, 128),
    "k1": (128, 128), "kr1": (16, 8, 128), "ks1": (8, 128), "z1": (128, 128),
    "k2": (256, 128), "kr2": (16, 16, 128), "ks2": (16, 128), "z2": (128, 128),
    "k3": (256, 128), "kr3": (8, 32, 128), "ks3": (32, 128), "z3": (128, 128),
    "ar4": (4, 96, 128), "ar3": (8, 48, 128), "ar2": (16, 24, 128),
    "am1": (192, 128), "ap1": (16, 12, 128), "ar1": (16, 12, 128),
    "am0": (96, 128), "ap0": (16, 6, 128), "ar0": (16, 6, 128),
}
for _way in "fb":
    for _l in range(LEVELS):
        _h = ROWS[_l] // 2
        SCRATCH[f"{_way}p{_l}"] = (2 * _h, 128)
        SCRATCH[f"{_way}c{_l}"] = (_h, 128)
        SCRATCH[f"{_way}h{_l}"] = (_h, 128)
        if _l >= 4:
            SCRATCH[f"{_way}r{_l}"] = (4, _h // 4, 128)
            SCRATCH[f"{_way}q{_l}"] = (_h // 4, 128)
            SCRATCH[f"{_way}g{_l}"] = (_h, 128)
        else:
            SCRATCH[f"{_way}r{_l}"] = (4, _h, 128)
            SCRATCH[f"{_way}g{_l}"] = (_h, 128)
        SCRATCH[f"{_way}y{_l}"] = (2 * _h, 128)
NAMES = tuple(SCRATCH)
SEMS = 128
MATRICES = {
    "g0x": (48, 384), "g1x": (96, 384), "g2": (192, 384), "g3": (384, 384), "g4": (768, 384),
    "q1x": (96, 128), "q2": (192, 256), "p3": (384, 384), "p4": (512, 768),
    "g0": (192, 384), "g1": (192, 384), "q1": (192, 128),
    "h0": (384, 192), "h1": (384, 192), "h2": (384, 192), "h3": (384, 384), "h4": (384, 768),
    "p1": (128, 192), "p2": (256, 192), "q3": (384, 384), "q4": (768, 512),
}
LOADED = tuple(MATRICES)[:9]


def split(values):
    high = values.astype(jnp.bfloat16)
    low = (values - high.astype(jnp.float32)).astype(jnp.bfloat16)
    return jnp.concatenate([high, low], axis=1)


def times(matrix, values):
    both = jnp.dot(matrix, split(values), preferred_element_type=jnp.float32)
    return both[:, :128] + both[:, 128:]


def rows_of(index, count):
    return pl.ds(pl.multiple_of(index * count, 8), count)


def total(ref):
    parts = [ref[j] for j in range(ref.shape[0])]
    while len(parts) > 1:
        parts = [parts[j] + parts[j + 1] for j in range(0, len(parts), 2)]
    return parts[0]


def kernel(added, *refs):
    stored_rights, refs = refs[:5], refs[5:]
    stored, refs = refs[:9], refs[9:]
    outs, refs = refs[:5], refs[5:]
    v = dict(zip(NAMES, refs[: len(NAMES)]))
    refs = refs[len(NAMES) :]
    m = dict(zip(MATRICES, refs[: len(MATRICES)]))
    rights, refs = refs[len(MATRICES) : len(MATRICES) + 5], refs[len(MATRICES) + 5 :]
    send_sems, recv_sems, load_sems = refs

    leaf = lax.axis_index("leaf")
    front = lax.axis_index("front")
    x, z = lax.div(leaf, NZ), lax.rem(leaf, NZ)
    y, core = lax.div(front, 2), lax.rem(front, 2)
    pair = lax.rem(x, 2)

    counter = [0]
    sent = []

    def each_z(n, act):
        here = lax.rem(z, n)
        start = leaf - here

        def partner(d):
            there = lax.rem(here + d, n)
            act(there, start + there)

        def step(k, _):
            partner(n // 2 - k)
            partner(n // 2 + k)
            return 0

        partner(n // 2)
        lax.fori_loop(1, n // 2, step, 0)

    def at_x(d):
        other = lax.rem(x + d, NX)
        return other, (other * NZ + z, front)

    x_mate = ((x + 1 - 2 * pair) * NZ + z, front)
    core_mate = (leaf, front + 1 - 2 * core)

    def at_y(d):
        other = lax.rem(y + d, NY)
        return other, (leaf, other * 2 + core)

    def begin():
        counter[0] += 1
        return counter[0] - 1

    def send(src, dst, k, device):
        pltpu.make_async_remote_copy(
            src_ref=src, dst_ref=dst, send_sem=send_sems.at[k], recv_sem=recv_sems.at[k],
            device_id=device, device_id_type=MESH,
        ).start()

    def await_bytes(like, k, sems):
        pltpu.make_async_copy(like, like, sems.at[k]).wait()

    def scatter_z(n, src, rows, dst):
        k = begin()
        whole_pieces = len(src.shape) > 2

        def piece(i):
            return src.at[i] if whole_pieces else src.at[rows_of(i, rows)]

        here = lax.rem(z, n)
        each_z(n, lambda there, device: send(piece(there), dst.at[here], k, (device, front)))
        dst[here] = src[here] if whole_pieces else src[rows_of(here, rows), :]
        like = dst.at[pl.ds(0, n - 1)]
        sent.append((like, k))
        return lambda: await_bytes(like, k, recv_sems)

    def gather_z(n, src, rows, dst):
        k = begin()
        whole_pieces = len(dst.shape) > 2
        here = lax.rem(z, n)
        spot = dst.at[here] if whole_pieces else dst.at[rows_of(here, rows)]

        each_z(n, lambda there, device: send(src, spot, k, (device, front)))
        if whole_pieces:
            dst[here] = src[...]
        else:
            dst[rows_of(here, rows), :] = src[...]
        like = dst.at[pl.ds(0, (n - 1) if whole_pieces else (n - 1) * rows)]
        sent.append((like, k))
        return lambda: await_bytes(like, k, recv_sems)

    def gather_xz(src, dst, slot, other_x):
        k, k_other = begin(), begin()

        def both(there, device):
            send(src, dst.at[slot, z], k_other, (other_x * NZ + there, front))
            send(src, dst.at[slot, z], k, (device, front))

        each_z(NZ, both)
        send(src, dst.at[slot, z], k_other, (other_x * NZ + z, front))
        dst[slot, z] = src[...]
        sent.append((dst.at[0, pl.ds(0, NZ - 1)], k))
        sent.append((dst.at[0], k_other))

        def done():
            await_bytes(dst.at[0, pl.ds(0, NZ - 1)], k, recv_sems)
            await_bytes(dst.at[0], k_other, recv_sems)

        return done

    def to_one(src, dst, device):
        k = begin()
        send(src, dst, k, device)
        sent.append((dst, k))
        return lambda: await_bytes(dst, k, recv_sems)

    def to_x(pieces, dst):
        k = begin()
        for d in (2, 1, 3):
            other, device = at_x(d)
            send(pieces(other), dst.at[x], k, device)
        like = dst.at[pl.ds(0, 3)]
        sent.append((like, k))
        return lambda: await_bytes(like, k, recv_sems)

    def to_y(pieces, spot, like):
        k = begin()
        for d in (2, 1, 3):
            other, device = at_y(d)
            send(pieces(other), spot, k, device)
        sent.append((like, k))
        return lambda: await_bytes(like, k, recv_sems)

    def front_sum(way, level, meanwhile=None):
        term, half, whole = v[f"{way}p{level}"], v[f"{way}h{level}"], v[f"{way}y{level}"]
        received, summed = v[f"{way}r{level}"], v[f"{way}g{level}"]
        h = ROWS[level] // 2
        from_core = v[f"{way}c{level}"]
        done = to_one(term.at[rows_of(1 - core, h)], from_core, core_mate)
        done()
        half[...] = term[rows_of(core, h), :] + from_core[...]
        if level >= 4:
            q = h // 4
            piece = v[f"{way}q{level}"]
            done = to_y(lambda other: half.at[rows_of(other, q)], received.at[y], received.at[pl.ds(0, 3)])
            received[y] = half[rows_of(y, q), :]
            if meanwhile is not None:
                meanwhile()
            done()
            piece[...] = total(received)
            done = to_y(lambda other: piece, summed.at[rows_of(y, q)], summed.at[pl.ds(0, 3 * q)])
            summed[rows_of(y, q), :] = piece[...]
            done()
        else:
            done = to_y(lambda other: half, received.at[y], received.at[pl.ds(0, 3)])
            received[y] = half[...]
            if meanwhile is not None:
                meanwhile()
            done()
            summed[...] = total(received)
        done = to_one(summed, whole.at[rows_of(core, h)], core_mate)
        whole[rows_of(core, h), :] = summed[...]
        done()
        return whole

    def choice(level, child):
        block = added[front, 0, 2 ** (level + 1) - 2 + child]
        return [jnp.where(block == j, 1.0, 0.0).astype(jnp.float32) for j in range(3)]

    def choices(level):
        node = leaf // (64 >> level)
        return choice(level, 2 * node), choice(level, 2 * node + 1)

    def place(level, b, low, high):
        to_low, to_high = choices(level)
        target = v[f"c{level}"]
        for j in range(3):
            spot = slice(j * B, (j + 1) * B)
            target[spot, :] = b[spot, :] - low * to_low[j] - high * to_high[j]

    def pick(s, weights):
        return s[0:B, :] * weights[0] + s[B : 2 * B, :] * weights[1] + s[2 * B :, :] * weights[2]

    loads = {}

    def load(name, src, dst, k):
        copy = pltpu.make_async_copy(src, dst, load_sems.at[k])
        copy.start()
        loads[name] = copy.wait

    load("r4", stored_rights[4].at[0, 0], rights[4], 4)
    load("g4", stored[4], m["g4"], 9)
    for level in (3, 2):
        load(f"r{level}", stored_rights[level].at[0, 0], rights[level], level)
    for level in (1, 0):
        for i in range(OWN[level]):
            pltpu.make_async_copy(
                stored_rights[level].at[0, i], rights[level].at[pl.ds(i, 1)], load_sems.at[level]
            ).start()
    for k, name in enumerate(LOADED):
        if name != "g4":
            load(name, stored[k], m[name], 5 + k)

    barrier = pltpu.get_barrier_semaphore()

    def greet(device):
        pl.semaphore_signal(barrier, inc=1, device_id=device, device_id_type=MESH)

    greet((x * NZ + (z + 4) % NZ, front))
    greet((x * NZ + (z + 12) % NZ, front))
    each_z(4, lambda there, device: greet((device, front)))
    for d in (1, 2, 3):
        greet(at_x(d)[1])
        greet(at_y(d)[1])
    greet(core_mate)
    pl.semaphore_wait(barrier, 12)

    loads["r4"]()
    done_b4 = gather_z(4, rights[4], 96, v["c4"])
    await_bytes(rights[1], 1, load_sems)
    await_bytes(rights[0], 0, load_sems)
    for name in ("r3", "r2") + LOADED:
        loads[name]()
    v["t0"][x] = m["g0x"][...].astype(jnp.float32)
    v["t1"][pair] = m["g1x"][...].astype(jnp.float32)
    v["tp"][pair] = m["q1x"][...].astype(jnp.float32)
    done_tiles = [
        to_x(lambda other: v["t0"].at[x], v["t0"]),
        to_one(v["t1"].at[pair], v["t1"].at[pair], x_mate),
        to_one(v["tp"].at[pair], v["tp"].at[pair], x_mate),
    ]
    done_b = {}

    def turn(*names):
        for source, target in names:
            m[target][...] = m[source][...].T

    def more_b3():
        done_b[3] = gather_z(8, rights[3], 48, v["b3"])

    def more_b2():
        done_b[2] = gather_z(NZ, rights[2], 24, v["b2"])

    def more_b1():
        done_b[1] = gather_z(NZ, rights[1], 12, v["b1"].at[pair])

    def more_b0():
        done_b[0] = gather_z(NZ, rights[0], 6, v["b0"].at[x])

    turn(("g4", "h4"))
    done_b4()
    v["fp4"][...] = times(m["g4"][...], v["c4"][...])
    y4 = front_sum("f", 4, more_b3)
    v["u4"][...] = times(m["p4"][...], y4[...])
    done = scatter_z(4, v["u4"], 32, v["ur4"])
    turn(("p4", "q4"))
    done()
    v["us4"][...] = total(v["ur4"])
    done = gather_z(8, v["us4"], 32, v["ug4"])
    turn(("g3", "h3"), ("q2", "p2"))
    done_b[3]()
    done()

    place(3, v["b3"], v["ug4"][0:B, :], v["ug4"][B:, :])
    v["fp3"][...] = times(m["g3"][...], v["c3"][...])
    y3 = front_sum("f", 3, more_b2)
    v["u3"][...] = times(m["p3"][...], y3[...]) + v["u4"][B:, :]
    done = scatter_z(8, v["u3"], 16, v["ur3"])
    turn(("p3", "q3"))
    done()
    v["us3"][...] = total(v["ur3"])
    done = gather_z(NZ, v["us3"], 16, v["ug3"])
    for wait in done_tiles:
        wait()
    m["g0"][...] = v["t0"][...].reshape(192, 384).astype(jnp.bfloat16)
    m["g1"][...] = v["t1"][...].reshape(192, 384).astype(jnp.bfloat16)
    m["q1"][...] = v["tp"][...].reshape(192, 128).astype(jnp.bfloat16)
    turn(("g2", "h2"), ("g1", "h1"), ("g0", "h0"), ("q1", "p1"))
    done_b[2]()
    done()

    place(2, v["b2"], v["ug3"][0:B, :], v["ug3"][B:, :])
    v["fp2"][...] = times(m["g2"][...], v["c2"][...])
    y2 = front_sum("f", 2, more_b1)
    v["u2"][...] = times(m["p2"][...], y2[...]) + v["u3"][B:, :]
    scatter_z(NZ, v["u2"], 8, v["ur2"])()
    v["us2"][...] = total(v["ur2"])
    done = gather_xz(v["us2"], v["ug2"], pair, x + 1 - 2 * pair)
    done_u2x = to_one(v["u2"].at[pl.ds(B, B)], v["u2x"], x_mate)
    done_b[1]()
    to_one(v["b1"].at[pair], v["b1"].at[pair], x_mate)()
    for p in range(32):
        v["c1"][12 * p : 12 * p + 12, :] = v["b1"][p // 16, p % 16]
    done()

    low, high = (v["ug2"][j].reshape(B, 128) for j in range(2))
    place(1, v["c1"], low, high)
    v["fp1"][...] = times(m["g1"][...], v["c1"][...])
    y1 = front_sum("f", 1, more_b0)
    done_u2x()
    v["u1"][...] = times(m["p1"][...], y1[...]) + (v["u2"][B:, :] + v["u2x"][...])
    scatter_z(NZ, v["u1"], 8, v["ur1"])()
    v["us1"][...] = total(v["ur1"])
    done = gather_xz(v["us1"], v["ug1"], x // 2, (x + 2) % NX)
    done_b[0]()
    to_x(lambda other: v["b0"].at[x], v["b0"])()
    for p in range(64):
        v["c0"][6 * p : 6 * p + 6, :] = v["b0"][p // 16, p % 16]
    done()

    low, high = (v["ug1"][j].reshape(B, 128) for j in range(2))
    place(0, v["c0"], low, high)
    v["fp0"][...] = times(m["g0"][...], v["c0"][...])
    y0 = front_sum("f", 0)

    def solve(level, right_side):
        v[f"s{level}"][...] = times(m[f"h{level}"][...], right_side)

    def picked(level):
        to_low, to_high = choices(level)
        s = v[f"s{level}"]
        return pick(s, to_low), pick(s, to_high)

    def remove(level, known, meanwhile=None):
        v[f"bp{level}"][...] = times(m[f"q{level}"][...], known)
        through = front_sum("b", level, meanwhile)
        return v[f"fy{level}"][...] - through[...]

    answers = {}
    solve(0, y0[...])
    v["k0"][...] = pick(v["s0"], choice(0, x // 2))
    scatter_z(NZ, v["k0"], 8, v["kr0"])()
    v["ks0"][...] = total(v["kr0"])
    gather_z(NZ, v["ks0"], 8, v["z0"])()
    known = v["z0"][...]

    def root_answer():
        v["am0"][...] = v["s0"][rows_of(x, 96), :]
        for p in range(16):
            v["ap0"][p] = v["am0"][6 * p : 6 * p + 6, :]
        answers[0] = scatter_z(NZ, v["ap0"], 6, v["ar0"])

    solve(1, remove(1, known, root_answer))
    v["k1"][...] = pick(v["s1"], choice(1, x))
    scatter_z(NZ, v["k1"], 8, v["kr1"])()
    v["ks1"][...] = total(v["kr1"])
    gather_z(NZ, v["ks1"], 8, v["z1"])()
    known = jnp.concatenate([v["z1"][...], known], 0)

    def first_answer():
        v["am1"][...] = v["s1"][rows_of(pair, 192), :]
        for p in range(16):
            v["ap1"][p] = v["am1"][12 * p : 12 * p + 12, :]
        answers[1] = scatter_z(NZ, v["ap1"], 12, v["ar1"])

    solve(2, remove(2, known, first_answer))
    for j, rows in enumerate(picked(2)):
        v["k2"][j * B : (j + 1) * B, :] = rows
    scatter_z(NZ, v["k2"], 16, v["kr2"])()
    v["ks2"][...] = total(v["kr2"])
    gather_z(8, v["ks2"], 16, v["z2"])()
    known = jnp.concatenate([v["z2"][...], known], 0)

    def second_answer():
        answers[2] = scatter_z(NZ, v["s2"], 24, v["ar2"])

    solve(3, remove(3, known, second_answer))
    for j, rows in enumerate(picked(3)):
        v["k3"][j * B : (j + 1) * B, :] = rows
    scatter_z(8, v["k3"], 32, v["kr3"])()
    v["ks3"][...] = total(v["kr3"])
    gather_z(4, v["ks3"], 32, v["z3"])()
    known = jnp.concatenate([v["z3"][...], known], 0)

    def third_answer():
        answers[3] = scatter_z(8, v["s3"], 48, v["ar3"])

    solve(4, remove(4, known, third_answer))
    answers[4] = scatter_z(4, v["s4"], 96, v["ar4"])
    for level in range(LEVELS):
        answers[level]()
        outs[level][0, 0] = total(v[f"ar{level}"])
    for like, k in sent:
        await_bytes(like, k, send_sems)


def per_device(added_rows, r0, r1, r2, r3, r4, g0, g1, g2, g3, g4, p1, p2, p3, p4):
    vmem = pl.BlockSpec(memory_space=pltpu.VMEM)
    return pl.pallas_call(
        kernel,
        out_shape=tuple(jax.ShapeDtypeStruct((1, 1, w, 128), jnp.float32) for w in OWN),
        in_specs=[pl.BlockSpec(memory_space=pltpu.SMEM)] + [pl.BlockSpec(memory_space=pl.ANY)] * 14,
        out_specs=(vmem,) * 5,
        scratch_shapes=[pltpu.VMEM(shape, jnp.float32) for shape in SCRATCH.values()]
        + [pltpu.VMEM(shape, jnp.bfloat16) for shape in MATRICES.values()]
        + [pltpu.VMEM((w, 128), jnp.float32) for w in OWN]
        + [pltpu.SemaphoreType.DMA((SEMS,)), pltpu.SemaphoreType.DMA((SEMS,)), pltpu.SemaphoreType.DMA((14,))],
        compiler_params=pltpu.CompilerParams(
            collective_id=0, has_side_effects=True, vmem_limit_bytes=57 * 2**20
        ),
        cost_estimate=pl.CostEstimate(flops=1_200_000_000, bytes_accessed=3_000_000, transcendentals=0),
        name="solve",
    )(added_rows.transpose(1, 2, 0), r0.transpose(0, 2, 1, 3), r1.transpose(0, 2, 1, 3), r2, r3, r4, g0, g1, g2, g3, g4, p1.T, p2.T, p3, p4)


def solution(mesh):
    rights, inverses, panels = P("front", "leaf", None, None), P("leaf", "front"), P("front", "leaf")
    return jax.shard_map(
        per_device,
        mesh=mesh,
        in_specs=(P(),) + (rights,) * 5 + (inverses,) * 5 + (panels,) * 4,
        out_specs=(rights,) * 5,
        check_vma=False,
    )
```
